128 devices in a mesh: row: 8 (over z_hi, y), col: 16 (over x, z_lo, core).
Axes of the slice: x: 4, y: 4, z: 4 (z_hi: 2, z_lo: 2; z = z_hi * 2 + z_lo), core: 2. Of those that a mesh axis runs over, the one named last changes fastest.
Arguments:
- mode_panel: bfloat16 [512, 3, 8, 8192], P('col', None, 'row'), may hold values from -6 to 6
- domain_sizes: int32 [128], replicated, may hold values from 256 to 768, as said below
- ghost_send: int32 [128, 2, 128], P(('row', 'col')), may hold values from 0 to 767, as said below
- neighbours: int32 [128, 16, 768], P(('row', 'col')), may hold values from 0 to 1024, as said below
- force_blocks: float32 [128, 3, 3, 16, 768], P(('row', 'col')), may hold values from -0.0024414062 to 0.0024414062
- bond_vectors: float32 [128, 3, 16, 768], P(('row', 'col')), may hold values from -1 to 1
Outputs:
- velocity: float32 [3, 512, 512], P(None, 'row', 'col')
The draws below stay inside these ranges and needn't reach their ends.
Inputs may be any that keep to these rules, and one draw needn't show every extreme that they name: `domain_sizes`: domains in atom order; the sizes of domains 2k and 2k+1 sum to 1024, and one domain holds exactly 768 atoms. `ghost_send`: every entry of row d is below domain_sizes[d]. `neighbours`: for atom i of domain d: entries below 768 are below domain_sizes[d]; 768 to 895 name the atoms that domain d-1 sends, the next 128 those that domain d+1 sends; 1024 is an empty slot. Used slots come first, each atom below its domain's size has at least 8 of them and the first atom of every domain has 16; the other positions have only empty slots.
All inputs are finite; a program needn't handle non-finite values.
Results may differ from the reference program's by a relative error of at most 0.0029.
Values may be sent and summed in bfloat16 or wider, within the bound.
A program may use at most 128 MiB of HBM per device.

```python
import jax
import jax.numpy as jnp
from jax import lax

MODES = 512
ATOMS_DEV = 512
NBR = 16
GHOST = 128
BLK = 32
DOMAINS = 128
NATOMS = 65536
CAP = 768
LOCAL = 8192
N_ROW = 8


def split_domains(key):
    key = jax.random.fold_in(key, 7)
    first_key, second_key = jax.random.split(key, 2)
    half_count = DOMAINS // 2
    spread = ATOMS_DEV // 2
    shifts = jax.random.randint(first_key, (half_count,), -spread, spread + 1)
    chosen = jax.random.randint(second_key, (), 0, half_count)
    shifts = jnp.where(jnp.arange(half_count) == chosen, spread, shifts)
    paired = jnp.stack([ATOMS_DEV + shifts, ATOMS_DEV - shifts], axis=1).reshape(DOMAINS)
    return paired.astype(jnp.int32)


def draw_domain_sizes(key, part):
    return split_domains(key)


def draw_ghost_send(key, part):
    sizes = split_domains(key)
    key = jax.random.fold_in(key, 11)
    return jax.random.randint(key, (DOMAINS, 2, GHOST), 0, sizes[:, None, None]).astype(jnp.int32)


def draw_neighbours(key, part):
    sizes = split_domains(key)
    key = jax.random.fold_in(key, 23)
    count_key, own_key, ghost_key, pick_key = jax.random.split(key, 4)
    shape = (DOMAINS, NBR, CAP)
    atom_pos = jnp.arange(CAP)[None, None, :]
    slot_pos = jnp.arange(NBR)[None, :, None]
    used = jax.random.randint(count_key, (DOMAINS, 1, CAP), NBR // 2, NBR + 1)
    used = jnp.where(atom_pos == 0, NBR, used)
    own_pick = jax.random.randint(own_key, shape, 0, sizes[:, None, None])
    ghost_pick = jax.random.randint(ghost_key, shape, CAP, CAP + 2 * GHOST)
    choose = jax.random.randint(pick_key, shape, 0, 5)
    entry = jnp.where(choose == 0, ghost_pick, own_pick)
    alive = (slot_pos < used) & (atom_pos < sizes[:, None, None])
    return jnp.where(alive, entry, CAP + 2 * GHOST).astype(jnp.int32)


def shard_levels(rng, dims, cuts, low, high):
    loudness, own = 1.0, jax.random.fold_in(rng, 6)
    for axis_at, shards_of in cuts:
        steps = jnp.exp(jax.random.uniform(jax.random.fold_in(own, axis_at), (shards_of,), jnp.float32, low / len(cuts), high / len(cuts)))
        loudness = loudness * jnp.repeat(steps, dims[axis_at] // shards_of).reshape([-1 if axis == axis_at else 1 for axis in range(len(dims))])
    return loudness


def noise(key, shape, scale, reach, shards=(), kind=jnp.bfloat16):
    loudness = shard_levels(key, shape, shards, -0.22, 0.18) if shards else 1.0
    entries = jax.random.normal(key, shape, jnp.float32) * scale * loudness
    return jnp.minimum(jnp.maximum(entries, -reach), reach).astype(kind)


def setup_inputs(seed: int = 0) -> dict:
    key_of = jax.random.split(jax.random.key(seed), 7)
    mode_panel = noise(key_of[0], (MODES, 3, N_ROW, LOCAL), 1.0, 6.0, ((0, 16), (2, 8)))
    domain_sizes = draw_domain_sizes(jax.random.fold_in(key_of[6], 71), 0)
    ghost_send = draw_ghost_send(jax.random.fold_in(key_of[6], 71), 0)
    neighbours = draw_neighbours(jax.random.fold_in(key_of[6], 71), 0)
    force_blocks = noise(key_of[4], (DOMAINS, 3, 3, NBR, CAP), (108 * NATOMS) ** -0.5, 0.0024414062, ((0, 128),), jnp.float32)
    bond_vectors = jnp.clip(jax.random.uniform(key_of[5], (DOMAINS, 3, NBR, CAP), jnp.float32, -1.0, 1.0) * shard_levels(key_of[5], (DOMAINS, 3, NBR, CAP), ((0, 128),), -0.4, 0.0), -1.0, 1.0)
    return {"mode_panel": mode_panel, "domain_sizes": domain_sizes, "ghost_send": ghost_send, "neighbours": neighbours, "force_blocks": force_blocks, "bond_vectors": bond_vectors}


def to_atoms(mode_panel):
    rounds = LOCAL // BLK
    shaped = mode_panel.reshape(MODES, 3, N_ROW, rounds, BLK)
    return shaped.transpose(0, 1, 3, 2, 4).reshape(MODES, 3, NATOMS)


def reference(mode_panel, domain_sizes, ghost_send, neighbours, force_blocks, bond_vectors):
    eigen = to_atoms(mode_panel)
    padded_eigen = jnp.concatenate([eigen, jnp.zeros((MODES, 3, CAP), eigen.dtype)], axis=2)
    starts = (jnp.cumsum(domain_sizes) - domain_sizes).astype(jnp.int32)
    position = jnp.arange(CAP, dtype=jnp.int32)

    def domain_rows(index):
        piece = lax.dynamic_slice_in_dim(padded_eigen, starts[index], CAP, 2)
        inside = position < domain_sizes[index]
        return jnp.where(inside[None, None, :], piece, jnp.zeros((), eigen.dtype))

    def contribution(running, index):
        domain = domain_rows(index)
        before = (index + DOMAINS - 1) % DOMAINS
        after = (index + 1) % DOMAINS
        from_before = jnp.take(domain_rows(before), ghost_send[before, 0], axis=2)
        from_after = jnp.take(domain_rows(after), ghost_send[after, 1], axis=2)
        extended = jnp.concatenate([domain, from_before, from_after, jnp.zeros((MODES, 3, 1), eigen.dtype)], axis=2)

        def pair_step(pair_sum, pair_index):
            moved = jnp.take(extended, neighbours[index, pair_index], axis=2).astype(jnp.float32)
            phi_pair = force_blocks[index, :, :, pair_index, :]
            mixed_sum = jnp.sum(phi_pair[None] * moved[:, None], axis=2)
            bond_pair = bond_vectors[index, :, pair_index, :]
            return pair_sum + bond_pair[:, None, None, :] * mixed_sum[None], None

        start_sum = jnp.zeros((3, MODES, 3, CAP), jnp.float32)
        pulled, _ = lax.scan(pair_step, start_sum, jnp.arange(NBR, dtype=jnp.int32))
        pulled = pulled.astype(jnp.bfloat16).astype(jnp.float32).reshape(3 * MODES, 3 * CAP)
        own_rows = domain.astype(jnp.float32).reshape(MODES, 3 * CAP)
        return running + jnp.dot(own_rows, pulled.T, preferred_element_type=jnp.float32), None

    total, _ = lax.scan(contribution, jnp.zeros((MODES, 3 * MODES), jnp.float32), jnp.arange(DOMAINS, dtype=jnp.int32))
    return total.reshape(MODES, 3, MODES).transpose(1, 0, 2)
```

```python
import jax
import jax.numpy as jnp
from jax import lax
from jax.experimental import pallas as pl
from jax.experimental.pallas import tpu as pltpu
from jax.sharding import PartitionSpec as P

MESH = pl.DeviceIdType.MESH
BF16 = jnp.bfloat16
F32 = jnp.float32

CHIPS = 64
CAP = 768
CHIP_ATOMS = 1024
HALF = 512
NBR = 16
GHOST = 128
LANE = 128
WROWS = 40
PITCH = 520
WHALF = LANE * WROWS
UNROLL = 8
FROM_PREV = 1024
OWN_AFTER = 1152
OWN_BEFORE = 1280
FROM_NEXT = 1408
ZERO_ROW = 1536
TABLE = 1544


def kernel(
    panel, sizes, ghosts, nbrs, force, bond, out,
    modes, table, t32, raw_f, raw_b, raw_n, raw_g, merged, merged_n,
    idx_v, idx_s, ghost_s, u32, weights, pulled, to_next, to_prev, gin,
    vkeep, vsend, vrecv, part1, send1, recv1, part2, recv2, part3, recv3, fin, fin_in,
    local_sem, raw_send, raw_recv, panel_send, panel_recv, fwd_send, fwd_recv,
    ghost_send_sem, ghost_recv_sem, gfwd_send, gfwd_recv,
    core_send, core_recv, s1_send, s1_recv, s2_send, s2_recv, s3_send, s3_recv,
    fin_send, fin_recv,
):
    r = lax.axis_index("row")
    c = lax.axis_index("col")
    s = lax.rem(c, 2)
    cp = c // 2
    me = r * 8 + cp
    zh, y = r // 4, lax.rem(r, 4)
    x, zl = cp // 2, lax.rem(cp, 2)
    z = zh * 2 + zl
    sib = (r, cp * 2 + 1 - s)

    def chip_device(k):
        return (k // 8, lax.rem(k, 8) * 2 + s)

    def lanes_of(k):
        return pl.ds(pl.multiple_of(k * LANE, LANE), LANE)

    def remote(src, dst, ssem, rsem, dev):
        return pltpu.make_async_remote_copy(
            src_ref=src, dst_ref=dst, send_sem=ssem, recv_sem=rsem,
            device_id=dev, device_id_type=MESH,
        )

    barrier = pltpu.get_barrier_semaphore()
    pl.semaphore_signal(barrier, inc=1, device_id=sib, device_id_type=MESH)
    across = (r, cp * 2 + 1 - s + 2 - 4 * zl)
    pl.semaphore_signal(barrier, inc=1, device_id=across, device_id_type=MESH)

    def greet(i, carry):
        k = lax.rem(me + i, CHIPS)
        pl.semaphore_signal(barrier, inc=1, device_id=chip_device(k), device_id_type=MESH)
        return carry

    lax.fori_loop(1, CHIPS, greet, 0)

    raws = ((force, raw_f), (bond, raw_b), (nbrs, raw_n), (ghosts, raw_g))
    own = [
        pltpu.make_async_copy(src, dst.at[s], local_sem.at[n])
        for n, (src, dst) in enumerate(raws)
    ]
    own.append(
        pltpu.make_async_copy(
            panel.at[:, :, lanes_of(me)], modes.at[:, cp, s, :, lanes_of(r)], local_sem.at[4]
        )
    )
    for copy in own:
        copy.start()
    zero8 = jnp.zeros((8, LANE), F32)

    def clear_w(i, carry):
        pulled[pl.ds(i * 8, 8), :] = zero8
        return carry

    lax.fori_loop(0, 2 * WHALF // 8, clear_w, 0)

    def clear_t(i, carry):
        t32[pl.ds(i * 8, 8), :] = zero8
        return carry

    lax.fori_loop(0, LANE * 16 // 8, clear_t, 0)
    for i in range(32):
        u32[pl.ds(i * 8, 8), :] = zero8
    table[pl.ds(ZERO_ROW, TABLE - ZERO_ROW)] = jnp.zeros((TABLE - ZERO_ROW, 16, LANE), BF16)
    pl.semaphore_wait(barrier, CHIPS + 1)

    raw_copies = [
        remote(src, dst.at[s], raw_send.at[n], raw_recv.at[n], sib)
        for n, (src, dst) in enumerate(raws)
    ]
    for copy in raw_copies:
        copy.start()

    def panel_copy(i):
        k = lax.rem(me + i, CHIPS)
        return remote(
            panel.at[:, :, lanes_of(k)], modes.at[:, cp, s, :, lanes_of(r)],
            panel_send.at[i], panel_recv.at[me], chip_device(k),
        )

    def panel_start(i, carry):
        panel_copy(i).start()
        return carry

    lax.fori_loop(1, CHIPS, panel_start, 0)
    for copy in own:
        copy.wait()
    for copy in raw_copies:
        copy.wait()
    ghost_copy = pltpu.make_async_copy(raw_g, ghost_s, local_sem.at[0])
    ghost_copy.start()

    n0 = sizes[2 * me]
    lane = lax.broadcasted_iota(jnp.int32, (8, CHIP_ATOMS), 1)
    first = lane < n0

    def merge(x0, x1):
        pad = jnp.zeros((8, CHIP_ATOMS - CAP), x0.dtype)
        a = jnp.concatenate([x0, pad], axis=1)
        b = pltpu.roll(jnp.concatenate([x1, pad], axis=1), n0, 1)
        return jnp.where(first, a, b)

    def merge_force(g, carry):
        rows = pl.ds(pl.multiple_of(g * 8, 8), 8)
        merged[rows, :] = merge(raw_f[0, rows, :], raw_f[1, rows, :])
        return carry

    def merge_bond(g, carry):
        rows = pl.ds(pl.multiple_of(g * 8, 8), 8)
        merged[pl.ds(pl.multiple_of(144 + g * 8, 8), 8), :] = merge(
            raw_b[0, rows, :], raw_b[1, rows, :]
        )
        return carry

    lax.fori_loop(0, 18, merge_force, 0)
    lax.fori_loop(0, 6, merge_bond, 0)
    for g in range(2):
        rows = pl.ds(g * 8, 8)
        merged_n[rows, :] = merge(raw_n[0, rows, :], raw_n[1, rows, :])
    for b in range(4):
        v = merged_n[:, lanes_of(2 * b + s)]
        pos = (2 * b + s) * LANE + lax.broadcasted_iota(jnp.int32, (NBR, LANE), 1)
        late = pos >= n0
        inner = v + jnp.where(late, n0, 0)
        outer = v + jnp.where(late, 512, 256)
        row = jnp.where(v < CAP, inner, jnp.where(v >= CHIP_ATOMS, ZERO_ROW, outer))
        idx_v[:, pl.ds(b * LANE, LANE)] = row
    idx_copy = pltpu.make_async_copy(idx_v, idx_s, local_sem.at[1])
    idx_copy.start()

    block_lane = lax.rem(lax.broadcasted_iota(jnp.int32, (LANE, LANE), 1), 4)

    def weights_block(b, carry):
        tile = lanes_of(2 * b + s)

        def one(ac, carry):
            a = ac // 3
            comp = lax.rem(ac, 3)
            bv = merged[pl.ds(pl.multiple_of(144 + a * 16, 16), 16), tile]
            for e in range(3):
                w = bv * merged[pl.ds(pl.multiple_of((comp * 3 + e) * 16, 16), 16), tile]
                for m in range(4):
                    for half in range(2):
                        u32[pl.ds(half * 128 + e * 4 + m, 8, stride=16), :] = w[half * 8 : half * 8 + 8]
            for half in range(2):
                t = u32[pl.ds(half * 128, 128), :].T
                for m in range(4):
                    tm = jnp.where(block_lane == m, t, 0.0)
                    for g in range(16):
                        pulled[pl.ds(half * WHALF + g * 8 * WROWS + ac * 4 + m, 8, stride=WROWS), :] = tm[g * 8 : g * 8 + 8]
            return carry

        lax.fori_loop(0, 9, one, 0)

        def pack(t, carry):
            for half in range(2):
                w = pulled[pl.ds(pl.multiple_of(half * WHALF + t * WROWS, 8), WROWS), :]
                high = w.astype(BF16).astype(F32)
                both = jnp.concatenate([high, w - high], axis=0).astype(BF16)
                weights[b * LANE + t, :, half * LANE : half * LANE + LANE] = both
            return carry

        lax.fori_loop(0, LANE, pack, 0, unroll=4)
        return carry

    lax.fori_loop(0, 4, weights_block, 0)
    ghost_copy.wait()
    idx_copy.wait()

    def forward_copy(rr):
        half = modes.at[:, :, s, :, lanes_of(rr)]
        return remote(half, half, fwd_send.at[rr], fwd_recv.at[rr], sib)

    def other_copy(rr):
        half = modes.at[:, :, 1 - s, :, lanes_of(rr)]
        return remote(half, half, fwd_send.at[rr], fwd_recv.at[rr], sib)

    def arrive(i):
        rr = lax.rem(r + 7 - i, 8)

        def wait_one(cc, carry):
            ks = rr * 8 + cc

            @pl.when(ks != me)
            def _():
                chunk = modes.at[:, cc, s, :, lanes_of(rr)]
                remote(chunk, chunk, panel_send.at[0], panel_recv.at[ks], sib).wait_recv()

            return carry

        lax.fori_loop(0, 8, wait_one, 0)
        forward_copy(rr).start()

    def build(i):
        rr = lax.rem(r + 7 - i, 8)
        other_copy(rr).wait_recv()
        for e in range(3):
            for xx in range(4):
                v = modes[e, 2 * xx : 2 * xx + 2, :, :, lanes_of(rr)]
                vt = v.reshape(LANE, LANE).astype(F32).T
                for g in range(16):
                    t32[pl.ds(g * 128 + e * 4 + xx, 8, stride=16), :] = vt[g * 8 : g * 8 + 8]
        for b in range(4):
            rows = t32[pl.ds(b * 512, 512), :].astype(BF16).reshape(32, 16, LANE)
            table[pl.ds(b * 256 + rr * 32, 32)] = rows

    arrive(0)

    def group(i, carry):
        arrive(i)
        build(i - 1)
        return carry

    lax.fori_loop(1, 8, group, 0)
    build(7)

    def pick(g, carry):
        gg = s * 64 + g
        to_next[g] = table[n0 + ghost_s[1, 0, gg]]
        to_prev[g] = table[ghost_s[0, 1, gg]]
        return carry

    lax.fori_loop(0, 64, pick, 0, unroll=8)
    nxt = chip_device(lax.rem(me + 1, CHIPS))
    prv = chip_device(lax.rem(me + CHIPS - 1, CHIPS))
    g_next = remote(to_next, gin.at[0, s], ghost_send_sem.at[0], ghost_recv_sem.at[0], nxt)
    g_prev = remote(to_prev, gin.at[1, s], ghost_send_sem.at[1], ghost_recv_sem.at[1], prv)
    g_next.start()
    g_prev.start()

    def pick_own(g, carry):
        table[OWN_AFTER + g] = table[n0 + ghost_s[1, 1, g]]
        table[OWN_BEFORE + g] = table[ghost_s[0, 0, g]]
        return carry

    lax.fori_loop(0, GHOST, pick_own, 0, unroll=8)
    shares = [
        remote(gin.at[n, s], gin.at[n, s], gfwd_send.at[n], gfwd_recv.at[n], sib) for n in range(2)
    ]
    g_next.wait_recv()
    shares[0].start()
    g_prev.wait_recv()
    shares[1].start()
    for n, base in ((0, FROM_PREV), (1, FROM_NEXT)):
        table[pl.ds(base + s * 64, 64)] = gin[n, s]
    for n, base in ((0, FROM_PREV), (1, FROM_NEXT)):
        remote(
            gin.at[n, 1 - s], gin.at[n, 1 - s], gfwd_send.at[n], gfwd_recv.at[n], sib
        ).wait_recv()
        table[pl.ds(base + (1 - s) * 64, 64)] = gin[n, 1 - s]

    def pull(n, carry):
        i0 = n * UNROLL
        b = i0 // LANE
        t0 = lax.rem(i0, LANE)
        q0 = (t0 // 32) * LANE + b * 32 + lax.rem(t0, 32)
        taken = [
            jnp.concatenate([table[idx_s[j, i0 + u]] for j in range(NBR)], axis=0)
            for u in range(UNROLL)
        ]
        sums = [
            jnp.dot(weights[i0 + u], taken[u], preferred_element_type=F32) for u in range(UNROLL)
        ]
        for u in range(UNROLL):
            for g in range(5):
                total = sums[u][g * 8 : g * 8 + 8] + sums[u][40 + g * 8 : 48 + g * 8]
                pulled[pl.ds(g * 8 * PITCH + q0 + u, 8, stride=PITCH), :] = total
        return carry

    lax.fori_loop(0, HALF // UNROLL, pull, 0)

    where = {"x": x, "y": y, "z": z}
    orders = ("xyz", "yzx", "zxy")

    def device_at(axis, j):
        if axis == "x":
            return (r, (j * 2 + zl) * 2 + s)
        if axis == "y":
            return (zh * 4 + j, c)
        return ((j // 2) * 4 + y, (x * 2 + lax.rem(j, 2)) * 2 + s)

    my_lanes = pl.ds(pl.multiple_of(s * HALF, HALF), HALF)

    def velocity(a):
        def part(n, carry):
            xp = n // 2
            zz = lax.rem(n, 2)
            acc = None
            for comp in range(3):
                row = (a * 3 + comp) * 4 + 2 * xp
                rhs = jnp.concatenate(
                    [
                        pulled[pl.ds(pl.multiple_of(row * PITCH, 8), HALF), :],
                        pulled[pl.ds(pl.multiple_of((row + 1) * PITCH, 8), HALF), :],
                    ],
                    axis=1,
                ).astype(BF16)
                lhs = modes[comp, pl.ds(zz * 4, 4), :, :, my_lanes].reshape(256, HALF)
                term = jnp.dot(lhs, rhs, preferred_element_type=F32)
                acc = term if acc is None else acc + term
            for yy in range(4):
                for ss in range(2):
                    for ll in range(2):
                        for xx in range(2):
                            at = (yy * 4 + ss * 2 + ll) * 16
                            block = acc[at : at + 16, xx * LANE : xx * LANE + LANE]
                            pos = {"x": 2 * xp + xx, "y": yy, "z": 2 * zz + ll}
                            p, q, t = (pos[axis] for axis in orders[a])
                            place = (p * 4 + q) * 4 + t
                            vkeep[a, ss, place] = block
                            vsend[a, ss, place] = block.astype(BF16)
            return carry

        lax.fori_loop(0, 4, part, 0)

    def core_copy(a):
        return remote(vsend.at[a, 1 - s], vrecv.at[a], core_send.at[a], core_recv.at[a], sib)

    def stage_copies(a, stage, src, dst, ssem, rsem, size):
        axis = orders[a][stage]
        mine = where[axis]
        copies = []
        for d in range(1, 4):
            j = lax.rem(mine + d, 4)
            copies.append(
                remote(
                    src.at[a, pl.ds(j * size, size)], dst.at[a, mine],
                    ssem.at[a, d - 1], rsem.at[a, mine], device_at(axis, j),
                )
            )
        return copies

    def stage_wait(a, stage, dst, rsem):
        axis = orders[a][stage]
        mine = where[axis]
        total = None
        for d in range(1, 4):
            j = lax.rem(mine + d, 4)
            remote(dst.at[a, j], dst.at[a, j], rsem.at[a, j], rsem.at[a, j], sib).wait_recv()
            term = dst[a, j].astype(F32)
            total = term if total is None else total + term
        return total

    def copies1(a):
        return stage_copies(a, 0, send1, recv1, s1_send, s1_recv, 16)

    def copies2(a):
        return stage_copies(a, 1, part2, recv2, s2_send, s2_recv, 4)

    def copies3(a):
        return stage_copies(a, 2, part3, recv3, s3_send, s3_recv, 1)

    def add1(a):
        core_copy(a).wait_recv()

        def step(n, carry):
            at = pl.ds(n * 8, 8)
            both = vkeep[a, s, at] + vrecv[a, at].astype(F32)
            part1[a, at] = both
            send1[a, at] = both.astype(BF16)
            return carry

        lax.fori_loop(0, 8, step, 0)
        for copy in copies1(a):
            copy.start()

    def add2(a):
        mine = where[orders[a][0]]
        total = part1[a, pl.ds(mine * 16, 16)] + stage_wait(a, 0, recv1, s1_recv)
        part2[a] = total
        for copy in copies2(a):
            copy.start()

    def add3(a):
        mine = where[orders[a][1]]
        total = part2[a, pl.ds(mine * 4, 4)] + stage_wait(a, 1, recv2, s2_recv)
        part3[a] = total
        for copy in copies3(a):
            copy.start()

    def add4(a):
        mine = where[orders[a][2]]
        total = part3[a, pl.ds(mine, 1)] + stage_wait(a, 2, recv3, s3_recv)
        fin[a] = total[0]

    velocity(0)
    core_copy(0).start()
    velocity(1)
    core_copy(1).start()
    add1(0)
    velocity(2)
    core_copy(2).start()
    add1(1)
    add1(2)
    for a in range(3):
        add2(a)
    for a in range(3):
        add3(a)
    for a in range(3):
        add4(a)

    slot = s * 2 + zl
    partners = ((0, 1), (1, 0), (1, 1))

    def partner(dz, ds):
        zz = jnp.where(dz == 1, 1 - zl, zl) if dz else zl
        ss = 1 - s if ds else s
        return (r, (x * 2 + zz) * 2 + ss), ss * 2 + zz

    fin_copies = []
    for n, (dz, ds) in enumerate(partners):
        dev, _ = partner(dz, ds)
        fin_copies.append(remote(fin, fin_in.at[slot], fin_send.at[n], fin_recv.at[slot], dev))
    for copy in fin_copies:
        copy.start()
    fin_in[slot] = fin[...]
    for dz, ds in partners:
        _, there = partner(dz, ds)
        remote(fin, fin_in.at[there], fin_recv.at[there], fin_recv.at[there], sib).wait_recv()
    shift = lax.rem(LANE - 32 * lax.rem(c, 4), LANE)
    for a in range(3):
        for n in range(4):
            out[a, pl.ds(n * 16, 16), :] = pltpu.roll(fin_in[n, a], shift, 1)[:, :32]

    def panel_done(i, carry):
        panel_copy(i).wait_send()
        return carry

    lax.fori_loop(1, CHIPS, panel_done, 0)

    def forward_done(i, carry):
        forward_copy(i).wait_send()
        return carry

    lax.fori_loop(0, 8, forward_done, 0)
    g_next.wait_send()
    g_prev.wait_send()
    for copy in shares:
        copy.wait_send()
    for a in range(3):
        core_copy(a).wait_send()
        for copy in copies1(a) + copies2(a) + copies3(a):
            copy.wait_send()
    for copy in fin_copies:
        copy.wait_send()


def body(mode_panel, domain_sizes, ghost_send, neighbours, force_blocks, bond_vectors):
    panel = mode_panel.transpose(1, 2, 0, 3).reshape(3, 32, 8192)
    any_spec = pl.BlockSpec(memory_space=pl.ANY)
    vm = pltpu.VMEM
    dma = pltpu.SemaphoreType.DMA
    return pl.pallas_call(
        kernel,
        out_shape=jax.ShapeDtypeStruct((3, 64, 32), F32),
        in_specs=[any_spec, pl.BlockSpec(memory_space=pltpu.SMEM)] + [any_spec] * 4,
        out_specs=pl.BlockSpec(memory_space=vm),
        scratch_shapes=[
            vm((3, 8, 2, 32, CHIP_ATOMS), BF16),
            vm((TABLE, 16, LANE), BF16),
            vm((LANE * 16, LANE), F32),
            vm((2, 144, CAP), F32),
            vm((2, 48, CAP), F32),
            vm((2, NBR, CAP), jnp.int32),
            vm((2, 2, GHOST), jnp.int32),
            vm((192, CHIP_ATOMS), F32),
            vm((NBR, CHIP_ATOMS), jnp.int32),
            vm((NBR, HALF), jnp.int32),
            pltpu.SMEM((NBR, HALF), jnp.int32),
            pltpu.SMEM((2, 2, GHOST), jnp.int32),
            vm((256, LANE), F32),
            vm((HALF, 2 * WROWS, 256), BF16),
            vm((40 * PITCH, LANE), F32),
            vm((64, 16, LANE), BF16),
            vm((64, 16, LANE), BF16),
            vm((2, 2, 64, 16, LANE), BF16),
            vm((3, 2, 64, 16, LANE), F32),
            vm((3, 2, 64, 16, LANE), BF16),
            vm((3, 64, 16, LANE), BF16),
            vm((3, 64, 16, LANE), F32),
            vm((3, 64, 16, LANE), BF16),
            vm((3, 4, 16, 16, LANE), BF16),
            vm((3, 16, 16, LANE), F32),
            vm((3, 4, 4, 16, LANE), F32),
            vm((3, 4, 16, LANE), F32),
            vm((3, 4, 1, 16, LANE), F32),
            vm((3, 16, LANE), F32),
            vm((4, 3, 16, LANE), F32),
            dma((5,)), dma((4,)), dma((4,)), dma((CHIPS,)), dma((CHIPS,)), dma((8,)), dma((8,)),
            dma((2,)), dma((2,)), dma((2,)), dma((2,)),
            dma((3,)), dma((3,)),
            dma((3, 3)), dma((3, 4)), dma((3, 3)), dma((3, 4)), dma((3, 3)), dma((3, 4)),
            dma((3,)), dma((4,)),
        ],
        compiler_params=pltpu.CompilerParams(
            collective_id=1, has_side_effects=True, vmem_limit_bytes=63 * 2**20
        ),
    )(
        panel,
        domain_sizes,
        ghost_send.reshape(2, 128),
        neighbours.reshape(16, 768),
        force_blocks.reshape(144, 768),
        bond_vectors.reshape(48, 768),
    )


def solution(mesh):
    return jax.shard_map(
        body,
        mesh=mesh,
        in_specs=(
            P("col", None, "row", None),
            P(),
            P(("row", "col"), None, None),
            P(("row", "col"), None, None),
            P(("row", "col"), None, None, None, None),
            P(("row", "col"), None, None, None),
        ),
        out_specs=P(None, "row", "col"),
        check_vma=False,
    )
```

```python
import jax
import jax.numpy as jnp
from jax import lax
from jax.experimental import pallas as pl
from jax.experimental.pallas import tpu as pltpu
from jax.sharding import PartitionSpec as P

MESH = pl.DeviceIdType.MESH
BF16 = jnp.bfloat16
F32 = jnp.float32

CHIPS = 64
CAP = 768
CHIP_ATOMS = 1024
HALF = 512
NBR = 16
GHOST = 128
LANE = 128
WROWS = 40
PITCH = 520
WHALF = LANE * WROWS
UNROLL = 32
STEP = 5
FROM_PREV = 1024
OWN_AFTER = 1152
OWN_BEFORE = 1280
FROM_NEXT = 1408
ZERO_ROW = 1536
TABLE = 1544


def kernel(
    panel, sizes, ghosts, nbrs, force, bond, out,
    modes, table, t32, raw_f, raw_b, raw_n, raw_g, merged, merged_n,
    idx_v, idx_s, ghost_s, u32, weights, pulled, to_next, to_prev, gin,
    vkeep, vsend, vrecv, part1, send1, recv1, part2, recv2, part3, recv3,
    local_sem, raw_send, raw_recv, panel_send, panel_recv, fwd_send, fwd_recv,
    ghost_send_sem, ghost_recv_sem, gfwd_send, gfwd_recv,
    core_send, core_recv, s1_send, s1_recv, s2_send, s2_recv, s3_send, s3_recv,
):
    r = lax.axis_index("row")
    c = lax.axis_index("col")
    s = lax.rem(c, 2)
    cp = c // 2
    me = r * 8 + cp
    zh, y = r // 4, lax.rem(r, 4)
    x, zl = cp // 2, lax.rem(cp, 2)
    z = zh * 2 + zl
    sib = (r, cp * 2 + 1 - s)

    def chip_device(k):
        return (k // 8, lax.rem(k, 8) * 2 + s)

    def lanes_of(k):
        return pl.ds(pl.multiple_of(k * LANE, LANE), LANE)

    def remote(src, dst, ssem, rsem, dev):
        return pltpu.make_async_remote_copy(
            src_ref=src, dst_ref=dst, send_sem=ssem, recv_sem=rsem,
            device_id=dev, device_id_type=MESH,
        )

    barrier = pltpu.get_barrier_semaphore()
    pl.semaphore_signal(barrier, inc=1, device_id=sib, device_id_type=MESH)

    def greet(i, carry):
        k = lax.rem(me + i, CHIPS)
        pl.semaphore_signal(barrier, inc=1, device_id=chip_device(k), device_id_type=MESH)
        return carry

    lax.fori_loop(1, CHIPS, greet, 0)

    raws = ((force, raw_f), (bond, raw_b), (nbrs, raw_n), (ghosts, raw_g))
    own = [
        pltpu.make_async_copy(src, dst.at[s], local_sem.at[n])
        for n, (src, dst) in enumerate(raws)
    ]
    own.append(
        pltpu.make_async_copy(
            panel.at[:, :, lanes_of(me)], modes.at[:, cp, s, :, lanes_of(r)], local_sem.at[4]
        )
    )
    for copy in own:
        copy.start()
    pl.semaphore_wait(barrier, CHIPS)

    raw_copies = [
        remote(src, dst.at[s], raw_send.at[n], raw_recv.at[n], sib)
        for n, (src, dst) in enumerate(raws)
    ]
    for copy in raw_copies:
        copy.start()

    def panel_copy(i):
        k = lax.rem(me + i * STEP, CHIPS)
        return remote(
            panel.at[:, :, lanes_of(k)], modes.at[:, cp, s, :, lanes_of(r)],
            panel_send.at[i], panel_recv.at[me], chip_device(k),
        )

    def panel_start(i, carry):
        panel_copy(i).start()
        return carry

    lax.fori_loop(1, CHIPS, panel_start, 0)
    zero8 = jnp.zeros((8, LANE), F32)

    def clear_w(i, carry):
        pulled[pl.ds(i * 8, 8), :] = zero8
        return carry

    lax.fori_loop(0, 2 * WHALF // 8, clear_w, 0)

    def clear_t(i, carry):
        t32[pl.ds(i * 8, 8), :] = zero8
        return carry

    lax.fori_loop(0, LANE * 16 // 8, clear_t, 0)
    for i in range(32):
        u32[pl.ds(i * 8, 8), :] = zero8
    table[pl.ds(ZERO_ROW, TABLE - ZERO_ROW)] = jnp.zeros((TABLE - ZERO_ROW, 16, LANE), BF16)
    for copy in own:
        copy.wait()
    for copy in raw_copies:
        copy.wait()
    ghost_copy = pltpu.make_async_copy(raw_g, ghost_s, local_sem.at[0])
    ghost_copy.start()

    n0 = sizes[2 * me]
    lane = lax.broadcasted_iota(jnp.int32, (8, CHIP_ATOMS), 1)
    first = lane < n0

    def merge(x0, x1):
        pad = jnp.zeros((8, CHIP_ATOMS - CAP), x0.dtype)
        a = jnp.concatenate([x0, pad], axis=1)
        b = pltpu.roll(jnp.concatenate([x1, pad], axis=1), n0, 1)
        return jnp.where(first, a, b)

    def merge_force(g, carry):
        rows = pl.ds(pl.multiple_of(g * 8, 8), 8)
        merged[rows, :] = merge(raw_f[0, rows, :], raw_f[1, rows, :])
        return carry

    def merge_bond(g, carry):
        rows = pl.ds(pl.multiple_of(g * 8, 8), 8)
        merged[pl.ds(pl.multiple_of(144 + g * 8, 8), 8), :] = merge(
            raw_b[0, rows, :], raw_b[1, rows, :]
        )
        return carry

    lax.fori_loop(0, 18, merge_force, 0)
    lax.fori_loop(0, 6, merge_bond, 0)
    for g in range(2):
        rows = pl.ds(g * 8, 8)
        merged_n[rows, :] = merge(raw_n[0, rows, :], raw_n[1, rows, :])
    for b in range(4):
        v = merged_n[:, lanes_of(2 * b + s)]
        pos = (2 * b + s) * LANE + lax.broadcasted_iota(jnp.int32, (NBR, LANE), 1)
        late = pos >= n0
        inner = v + jnp.where(late, n0, 0)
        outer = v + jnp.where(late, 512, 256)
        row = jnp.where(v < CAP, inner, jnp.where(v >= CHIP_ATOMS, ZERO_ROW, outer))
        wide = jnp.concatenate([row, jnp.zeros((LANE - NBR, LANE), jnp.int32)], axis=0)
        idx_v[pl.ds(b * LANE, LANE), :] = wide.T
    idx_copy = pltpu.make_async_copy(idx_v, idx_s, local_sem.at[1])
    idx_copy.start()

    block_lane = lax.rem(lax.broadcasted_iota(jnp.int32, (LANE, LANE), 1), 4)

    def weights_block(b, carry):
        tile = lanes_of(2 * b + s)

        def one(ac, carry):
            a = ac // 3
            comp = lax.rem(ac, 3)
            bv = merged[pl.ds(pl.multiple_of(144 + a * 16, 16), 16), tile]
            for e in range(3):
                w = bv * merged[pl.ds(pl.multiple_of((comp * 3 + e) * 16, 16), 16), tile]
                for m in range(4):
                    for half in range(2):
                        u32[pl.ds(half * 128 + e * 4 + m, 8, stride=16), :] = w[half * 8 : half * 8 + 8]
            for half in range(2):
                t = u32[pl.ds(half * 128, 128), :].T
                for m in range(4):
                    tm = jnp.where(block_lane == m, t, 0.0)
                    for g in range(16):
                        pulled[pl.ds(half * WHALF + g * 8 * WROWS + ac * 4 + m, 8, stride=WROWS), :] = tm[g * 8 : g * 8 + 8]
            return carry

        lax.fori_loop(0, 9, one, 0)

        def pack(t, carry):
            for half in range(2):
                w = pulled[pl.ds(pl.multiple_of(half * WHALF + t * WROWS, 8), WROWS), :]
                high = w.astype(BF16).astype(F32)
                both = jnp.concatenate([high, w - high], axis=0).astype(BF16)
                weights[b * LANE + t, :, half * LANE : half * LANE + LANE] = both
            return carry

        lax.fori_loop(0, LANE, pack, 0, unroll=4)
        return carry

    lax.fori_loop(0, 4, weights_block, 0)
    ghost_copy.wait()
    idx_copy.wait()

    def forward_copy(rr):
        half = modes.at[:, :, s, :, lanes_of(rr)]
        return remote(half, half, fwd_send.at[rr], fwd_recv.at[rr], sib)

    def other_copy(rr):
        half = modes.at[:, :, 1 - s, :, lanes_of(rr)]
        return remote(half, half, fwd_send.at[rr], fwd_recv.at[rr], sib)

    def arrive(i):
        rr = lax.rem(r + 7 - i, 8)

        def wait_one(cc, carry):
            ks = rr * 8 + cc

            @pl.when(ks != me)
            def _():
                chunk = modes.at[:, cc, s, :, lanes_of(rr)]
                remote(chunk, chunk, panel_send.at[0], panel_recv.at[ks], sib).wait_recv()

            return carry

        lax.fori_loop(0, 8, wait_one, 0)
        forward_copy(rr).start()

    def build(i):
        rr = lax.rem(r + 7 - i, 8)
        other_copy(rr).wait_recv()
        for e in range(3):
            for xx in range(4):
                v = modes[e, 2 * xx : 2 * xx + 2, :, :, lanes_of(rr)]
                vt = v.reshape(LANE, LANE).astype(F32).T
                for g in range(16):
                    t32[pl.ds(g * 128 + e * 4 + xx, 8, stride=16), :] = vt[g * 8 : g * 8 + 8]
        for b in range(4):
            rows = t32[pl.ds(b * 512, 512), :].astype(BF16).reshape(32, 16, LANE)
            table[pl.ds(b * 256 + rr * 32, 32)] = rows

    arrive(0)

    def group(i, carry):
        arrive(i)
        build(i - 1)
        return carry

    lax.fori_loop(1, 8, group, 0)
    build(7)

    three = lax.broadcasted_iota(jnp.int32, (48, 64), 0)
    four = lax.broadcasted_iota(jnp.int32, (48, 64), 1)
    part_of = three // 16
    kept = (part_of * 16 + lax.rem(three, 16) == four) & (lax.rem(three, 16) < 12)
    moved = (48 + part_of * 4 + lax.rem(three, 16) - 12 == four) & (lax.rem(three, 16) >= 12)
    shut = jnp.where(kept | moved, 1.0, 0.0)
    open_up = shut.T.astype(BF16)
    shut = shut.astype(BF16)

    def pack_rows(rows):
        return jnp.dot(shut, jnp.concatenate(rows, axis=0), preferred_element_type=F32).astype(BF16)

    nxt = chip_device(lax.rem(me + 1, CHIPS))
    prv = chip_device(lax.rem(me + CHIPS - 1, CHIPS))

    def ghost_copy_of(n, h):
        piece = pl.ds(h * 8, 8)
        return remote(
            (to_next, to_prev)[n].at[piece], gin.at[n, s, piece],
            ghost_send_sem.at[n, h], ghost_recv_sem.at[n, h], (nxt, prv)[n],
        )

    def share_copy_of(n, h, half):
        piece = gin.at[n, half, pl.ds(h * 8, 8)]
        return remote(piece, piece, gfwd_send.at[n, h], gfwd_recv.at[n, h], sib)

    pieces = [(n, h) for h in range(2) for n in range(2)]

    def pick(g, carry):
        g0 = s * 64 + g * 4
        to_next[g] = pack_rows([table[n0 + ghost_s[1, 0, g0 + u]] for u in range(4)])
        to_prev[g] = pack_rows([table[ghost_s[0, 1, g0 + u]] for u in range(4)])
        return carry

    for h in range(2):
        lax.fori_loop(h * 8, h * 8 + 8, pick, 0, unroll=8)
        for n in range(2):
            ghost_copy_of(n, h).start()

    def pick_own(g, carry):
        table[OWN_AFTER + g] = table[n0 + ghost_s[1, 1, g]]
        table[OWN_BEFORE + g] = table[ghost_s[0, 0, g]]
        return carry

    lax.fori_loop(0, GHOST, pick_own, 0, unroll=8)

    def unpack(n, h, half):
        base = (FROM_PREV, FROM_NEXT)[n] + half * 64 + h * 32

        def step(g, carry):
            rows = jnp.dot(open_up, gin[n, half, h * 8 + g], preferred_element_type=F32)
            table[pl.ds(base + g * 4, 4)] = rows.astype(BF16).reshape(4, 16, LANE)
            return carry

        lax.fori_loop(0, 8, step, 0, unroll=8)

    for n, h in pieces:
        ghost_copy_of(n, h).wait_recv()
        share_copy_of(n, h, s).start()
        unpack(n, h, s)
    for n, h in pieces:
        share_copy_of(n, h, 1 - s).wait_recv()
        unpack(n, h, 1 - s)

    def pull(n, carry):
        i0 = n * UNROLL
        b = i0 // LANE
        t0 = lax.rem(i0, LANE)
        q0 = (t0 // 32) * LANE + b * 32 + lax.rem(t0, 32)
        taken = [
            jnp.concatenate([table[idx_s[i0 + u, j]] for j in range(NBR)], axis=0)
            for u in range(UNROLL)
        ]
        sums = [
            jnp.dot(weights[i0 + u], taken[u], preferred_element_type=F32) for u in range(UNROLL)
        ]
        for u in range(UNROLL):
            for g in range(5):
                total = sums[u][g * 8 : g * 8 + 8] + sums[u][40 + g * 8 : 48 + g * 8]
                pulled[pl.ds(g * 8 * PITCH + q0 + u, 8, stride=PITCH), :] = total
        return carry

    lax.fori_loop(0, HALF // UNROLL, pull, 0)

    where = {"x": x, "y": y, "z": z}
    orders = ("xyz", "yzx", "zxy")

    def device_at(axis, j):
        if axis == "x":
            return (r, (j * 2 + zl) * 2 + s)
        if axis == "y":
            return (zh * 4 + j, c)
        return ((j // 2) * 4 + y, (x * 2 + lax.rem(j, 2)) * 2 + s)

    my_lanes = pl.ds(pl.multiple_of(s * HALF, HALF), HALF)

    lane_group = lax.broadcasted_iota(jnp.int32, (16, LANE), 1) // 32
    low = lane_group < 2
    even = lax.rem(lane_group, 2) == 0

    def velocity(a):
        def part(n, carry):
            xp = n // 2
            zz = lax.rem(n, 2)
            acc = None
            for comp in range(3):
                row = (a * 3 + comp) * 4 + 2 * xp
                rhs = jnp.concatenate(
                    [
                        pulled[pl.ds(pl.multiple_of(row * PITCH, 8), HALF), :],
                        pulled[pl.ds(pl.multiple_of((row + 1) * PITCH, 8), HALF), :],
                    ],
                    axis=1,
                ).astype(BF16)
                lhs = modes[comp, pl.ds(zz * 4, 4), :, :, my_lanes].reshape(256, HALF)
                term = jnp.dot(lhs, rhs, preferred_element_type=F32)
                acc = term if acc is None else acc + term
            for yy in range(4):
                for xx in range(2):
                    at = yy * 64
                    rows = [
                        acc[at + 16 * g : at + 16 * g + 16, xx * LANE : xx * LANE + LANE]
                        for g in range(4)
                    ]
                    halves = [None] * 4
                    for g in range(2):
                        halves[g] = jnp.where(low, rows[g], pltpu.roll(rows[g + 2], 64, 1))
                        halves[g + 2] = jnp.where(low, pltpu.roll(rows[g], 64, 1), rows[g + 2])
                    quarters = [None] * 4
                    for g in (0, 2):
                        quarters[g] = jnp.where(even, halves[g], pltpu.roll(halves[g + 1], 32, 1))
                        quarters[g + 1] = jnp.where(even, pltpu.roll(halves[g], 96, 1), halves[g + 1])
                    for quarter, block in enumerate(quarters):
                        ll, ss = divmod(quarter, 2)
                        pos = {"x": 2 * xp + xx, "y": yy, "z": 2 * zz + ll}
                        p, q, t = (pos[axis] for axis in orders[a])
                        place = (p * 4 + q) * 4 + t
                        vkeep[a, ss, place] = block
                        vsend[a, ss, place] = block.astype(BF16)
            return carry

        lax.fori_loop(0, 4, part, 0)

    def core_copy(a):
        return remote(vsend.at[a, 1 - s], vrecv.at[a], core_send.at[a], core_recv.at[a], sib)

    def stage_copies(a, stage, src, dst, ssem, rsem, size):
        axis = orders[a][stage]
        mine = where[axis]
        copies = []
        for d in range(1, 4):
            j = lax.rem(mine + d, 4)
            copies.append(
                remote(
                    src.at[a, pl.ds(j * size, size)], dst.at[a, mine],
                    ssem.at[a, d - 1], rsem.at[a, mine], device_at(axis, j),
                )
            )
        return copies

    def stage_wait(a, stage, dst, rsem):
        axis = orders[a][stage]
        mine = where[axis]
        total = None
        for d in range(1, 4):
            j = lax.rem(mine + d, 4)
            remote(dst.at[a, j], dst.at[a, j], rsem.at[a, j], rsem.at[a, j], sib).wait_recv()
            term = dst[a, j].astype(F32)
            total = term if total is None else total + term
        return total

    def copies1(a):
        return stage_copies(a, 0, send1, recv1, s1_send, s1_recv, 16)

    def copies2(a):
        return stage_copies(a, 1, part2, recv2, s2_send, s2_recv, 4)

    def copies3(a):
        return stage_copies(a, 2, part3, recv3, s3_send, s3_recv, 1)

    def add1(a):
        core_copy(a).wait_recv()

        def step(n, carry):
            at = pl.ds(n * 8, 8)
            both = vkeep[a, s, at] + vrecv[a, at].astype(F32)
            part1[a, at] = both
            send1[a, at] = both.astype(BF16)
            return carry

        lax.fori_loop(0, 8, step, 0)
        for copy in copies1(a):
            copy.start()

    def add2(a):
        mine = where[orders[a][0]]
        total = part1[a, pl.ds(mine * 16, 16)] + stage_wait(a, 0, recv1, s1_recv)
        part2[a] = total
        for copy in copies2(a):
            copy.start()

    def add3(a):
        mine = where[orders[a][1]]
        total = part2[a, pl.ds(mine * 4, 4)] + stage_wait(a, 1, recv2, s2_recv)
        part3[a] = total
        for copy in copies3(a):
            copy.start()

    def add4(a):
        mine = where[orders[a][2]]
        total = part3[a, pl.ds(mine, 1)] + stage_wait(a, 2, recv3, s3_recv)
        for g in range(4):
            out[a, pl.ds(g * 16, 16), :] = total[0][:, g * 32 : g * 32 + 32]

    velocity(0)
    core_copy(0).start()
    velocity(1)
    core_copy(1).start()
    add1(0)
    velocity(2)
    core_copy(2).start()
    add1(1)
    add1(2)
    for a in range(3):
        add2(a)
    for a in range(3):
        add3(a)
    for a in range(3):
        add4(a)

    def panel_done(i, carry):
        panel_copy(i).wait_send()
        return carry

    lax.fori_loop(1, CHIPS, panel_done, 0)

    def forward_done(i, carry):
        forward_copy(i).wait_send()
        return carry

    lax.fori_loop(0, 8, forward_done, 0)
    for n, h in pieces:
        ghost_copy_of(n, h).wait_send()
        share_copy_of(n, h, s).wait_send()
    for a in range(3):
        core_copy(a).wait_send()
        for copy in copies1(a) + copies2(a) + copies3(a):
            copy.wait_send()


def body(mode_panel, domain_sizes, ghost_send, neighbours, force_blocks, bond_vectors):
    panel = mode_panel.transpose(1, 2, 0, 3).reshape(3, 32, 8192)
    any_spec = pl.BlockSpec(memory_space=pl.ANY)
    vm = pltpu.VMEM
    dma = pltpu.SemaphoreType.DMA
    return pl.pallas_call(
        kernel,
        out_shape=jax.ShapeDtypeStruct((3, 64, 32), F32),
        in_specs=[any_spec, pl.BlockSpec(memory_space=pltpu.SMEM)] + [any_spec] * 4,
        out_specs=pl.BlockSpec(memory_space=vm),
        scratch_shapes=[
            vm((3, 8, 2, 32, CHIP_ATOMS), BF16),
            vm((TABLE, 16, LANE), BF16),
            vm((LANE * 16, LANE), F32),
            vm((2, 144, CAP), F32),
            vm((2, 48, CAP), F32),
            vm((2, NBR, CAP), jnp.int32),
            vm((2, 2, GHOST), jnp.int32),
            vm((192, CHIP_ATOMS), F32),
            vm((NBR, CHIP_ATOMS), jnp.int32),
            vm((HALF, LANE), jnp.int32),
            pltpu.SMEM((HALF, LANE), jnp.int32),
            pltpu.SMEM((2, 2, GHOST), jnp.int32),
            vm((256, LANE), F32),
            vm((HALF, 2 * WROWS, 256), BF16),
            vm((40 * PITCH, LANE), F32),
            vm((16, 48, LANE), BF16),
            vm((16, 48, LANE), BF16),
            vm((2, 2, 16, 48, LANE), BF16),
            vm((3, 2, 64, 16, LANE), F32),
            vm((3, 2, 64, 16, LANE), BF16),
            vm((3, 64, 16, LANE), BF16),
            vm((3, 64, 16, LANE), F32),
            vm((3, 64, 16, LANE), BF16),
            vm((3, 4, 16, 16, LANE), BF16),
            vm((3, 16, 16, LANE), F32),
            vm((3, 4, 4, 16, LANE), F32),
            vm((3, 4, 16, LANE), F32),
            vm((3, 4, 1, 16, LANE), F32),
            dma((5,)), dma((4,)), dma((4,)), dma((CHIPS,)), dma((CHIPS,)), dma((CHIPS,)), dma((CHIPS,)),
            dma((2, 2)), dma((2, 2)), dma((2, 2)), dma((2, 2)),
            dma((3,)), dma((3,)),
            dma((3, 3)), dma((3, 4)), dma((3, 3)), dma((3, 4)), dma((3, 3)), dma((3, 4)),
        ],
        compiler_params=pltpu.CompilerParams(
            collective_id=1, has_side_effects=True, vmem_limit_bytes=63 * 2**20
        ),
    )(
        panel,
        domain_sizes,
        ghost_send.reshape(2, 128),
        neighbours.reshape(16, 768),
        force_blocks.reshape(144, 768),
        bond_vectors.reshape(48, 768),
    )


def solution(mesh):
    return jax.shard_map(
        body,
        mesh=mesh,
        in_specs=(
            P("col", None, "row", None),
            P(),
            P(("row", "col"), None, None),
            P(("row", "col"), None, None),
            P(("row", "col"), None, None, None, None),
            P(("row", "col"), None, None, None),
        ),
        out_specs=P(None, "row", "col"),
        check_vma=False,
    )
```

```python
import jax
import jax.numpy as jnp
from jax import lax
from jax.experimental import pallas as pl
from jax.experimental.pallas import tpu as pltpu
from jax.sharding import PartitionSpec as P

MESH = pl.DeviceIdType.MESH
BF16 = jnp.bfloat16
F32 = jnp.float32

CHIPS = 64
CAP = 768
CHIP_ATOMS = 1024
HALF = 512
NBR = 16
GHOST = 128
LANE = 128
WROWS = 40
PITCH = 520
WHALF = LANE * WROWS
UNROLL = 32
STEP = 5
FROM_PREV = 1024
OWN_AFTER = 1152
OWN_BEFORE = 1280
FROM_NEXT = 1408
ZERO_ROW = 1536
TABLE = 1544


def kernel(
    panel, sizes, ghosts, nbrs, force, bond, out,
    modes, table, wide, raw_f, raw_b, raw_n, raw_g, merged, merged_n,
    idx_v, idx_a, idx_b, ghost_s, u32, weights, pulled, to_next, to_prev, gin,
    vkeep, vsend, vrecv, part1, send1, recv1, part2, recv2, part3, recv3,
    local_sem, raw_send, raw_recv, panel_send, panel_recv, fwd_send, fwd_recv,
    ghost_send_sem, ghost_recv_sem, gfwd_send, gfwd_recv,
    core_send, core_recv, s1_send, s1_recv, s2_send, s2_recv, s3_send, s3_recv,
):
    r = lax.axis_index("row")
    c = lax.axis_index("col")
    s = lax.rem(c, 2)
    cp = c // 2
    me = r * 8 + cp
    zh, y = r // 4, lax.rem(r, 4)
    x, zl = cp // 2, lax.rem(cp, 2)
    z = zh * 2 + zl
    sib = (r, cp * 2 + 1 - s)

    def chip_device(k):
        return (k // 8, lax.rem(k, 8) * 2 + s)

    def lanes_of(k):
        return pl.ds(pl.multiple_of(k * LANE, LANE), LANE)

    def remote(src, dst, ssem, rsem, dev):
        return pltpu.make_async_remote_copy(
            src_ref=src, dst_ref=dst, send_sem=ssem, recv_sem=rsem,
            device_id=dev, device_id_type=MESH,
        )

    barrier = pltpu.get_barrier_semaphore()
    pl.semaphore_signal(barrier, inc=1, device_id=sib, device_id_type=MESH)

    def greet(i, carry):
        k = lax.rem(me + i, CHIPS)
        pl.semaphore_signal(barrier, inc=1, device_id=chip_device(k), device_id_type=MESH)
        return carry

    lax.fori_loop(1, CHIPS, greet, 0)

    raws = ((force, raw_f), (bond, raw_b), (nbrs, raw_n), (ghosts, raw_g))
    own = [
        pltpu.make_async_copy(src, dst.at[s], local_sem.at[n])
        for n, (src, dst) in enumerate(raws)
    ]
    own.append(
        pltpu.make_async_copy(
            panel.at[:, :, lanes_of(me)], modes.at[:, cp, s, :, lanes_of(r)], local_sem.at[4]
        )
    )
    for copy in own:
        copy.start()
    pl.semaphore_wait(barrier, CHIPS)

    raw_copies = [
        remote(src, dst.at[s], raw_send.at[n], raw_recv.at[n], sib)
        for n, (src, dst) in enumerate(raws)
    ]
    for copy in raw_copies:
        copy.start()

    def panel_copy(i):
        k = lax.rem(me + i * STEP, CHIPS)
        return remote(
            panel.at[:, :, lanes_of(k)], modes.at[:, cp, s, :, lanes_of(r)],
            panel_send.at[i], panel_recv.at[me], chip_device(k),
        )

    def panel_start(i, carry):
        panel_copy(i).start()
        return carry

    lax.fori_loop(1, CHIPS, panel_start, 0)
    zero8 = jnp.zeros((8, LANE), F32)

    def clear_w(i, carry):
        pulled[pl.ds(i * 8, 8), :] = zero8
        return carry

    lax.fori_loop(0, 2 * WHALF // 8, clear_w, 0)

    for i in range(32):
        u32[pl.ds(i * 8, 8), :] = zero8
    table[pl.ds(ZERO_ROW, TABLE - ZERO_ROW)] = jnp.zeros((TABLE - ZERO_ROW, 16, LANE), BF16)
    for copy in own:
        copy.wait()
    for copy in raw_copies:
        copy.wait()
    ghost_copy = pltpu.make_async_copy(raw_g, ghost_s, local_sem.at[0])
    ghost_copy.start()

    n0 = sizes[2 * me]
    lane = lax.broadcasted_iota(jnp.int32, (8, CHIP_ATOMS), 1)
    first = lane < n0

    def merge(x0, x1):
        pad = jnp.zeros((8, CHIP_ATOMS - CAP), x0.dtype)
        a = jnp.concatenate([x0, pad], axis=1)
        b = pltpu.roll(jnp.concatenate([x1, pad], axis=1), n0, 1)
        return jnp.where(first, a, b)

    def merge_force(g, carry):
        rows = pl.ds(pl.multiple_of(g * 8, 8), 8)
        merged[rows, :] = merge(raw_f[0, rows, :], raw_f[1, rows, :])
        return carry

    def merge_bond(g, carry):
        rows = pl.ds(pl.multiple_of(g * 8, 8), 8)
        merged[pl.ds(pl.multiple_of(144 + g * 8, 8), 8), :] = merge(
            raw_b[0, rows, :], raw_b[1, rows, :]
        )
        return carry

    lax.fori_loop(0, 18, merge_force, 0)
    lax.fori_loop(0, 6, merge_bond, 0)
    for g in range(2):
        rows = pl.ds(g * 8, 8)
        merged_n[rows, :] = merge(raw_n[0, rows, :], raw_n[1, rows, :])
    for b in range(4):
        v = merged_n[:, lanes_of(2 * b + s)]
        pos = (2 * b + s) * LANE + lax.broadcasted_iota(jnp.int32, (NBR, LANE), 1)
        late = pos >= n0
        inner = v + jnp.where(late, n0, 0)
        outer = v + jnp.where(late, 512, 256)
        row = jnp.where(v < CAP, inner, jnp.where(v >= CHIP_ATOMS, ZERO_ROW, outer))
        square = jnp.concatenate([row, jnp.zeros((LANE - NBR, LANE), jnp.int32)], axis=0)
        idx_v[pl.ds(b * LANE, LANE), :] = square.T

    block_lane = lax.rem(lax.broadcasted_iota(jnp.int32, (LANE, LANE), 1), 4)

    def weights_block(b, carry):
        tile = lanes_of(2 * b + s)

        def one(ac, carry):
            a = ac // 3
            comp = lax.rem(ac, 3)
            bv = merged[pl.ds(pl.multiple_of(144 + a * 16, 16), 16), tile]
            for e in range(3):
                w = bv * merged[pl.ds(pl.multiple_of((comp * 3 + e) * 16, 16), 16), tile]
                for m in range(4):
                    for half in range(2):
                        u32[pl.ds(half * 128 + e * 4 + m, 8, stride=16), :] = w[half * 8 : half * 8 + 8]
            for half in range(2):
                t = u32[pl.ds(half * 128, 128), :].T
                for m in range(4):
                    tm = jnp.where(block_lane == m, t, 0.0)
                    for g in range(16):
                        pulled[pl.ds(half * WHALF + g * 8 * WROWS + ac * 4 + m, 8, stride=WROWS), :] = tm[g * 8 : g * 8 + 8]
            return carry

        lax.fori_loop(0, 9, one, 0)

        def pack(t, carry):
            for half in range(2):
                w = pulled[pl.ds(pl.multiple_of(half * WHALF + t * WROWS, 8), WROWS), :]
                high = w.astype(BF16).astype(F32)
                both = jnp.concatenate([high, w - high], axis=0).astype(BF16)
                weights[b * LANE + t, :, half * LANE : half * LANE + LANE] = both
            return carry

        lax.fori_loop(0, LANE, pack, 0, unroll=4)
        return carry

    lax.fori_loop(0, 4, weights_block, 0)
    ghost_copy.wait()

    def index_copy(n, slot):
        return pltpu.make_async_copy(
            idx_v.at[pl.ds(pl.multiple_of(n * UNROLL, UNROLL), UNROLL)],
            (idx_a, idx_b)[slot], local_sem.at[slot],
        )

    def clear_rows(i, carry):
        wide[i, pl.ds(12, 4), :] = jnp.zeros((4, LANE), F32)
        return carry

    lax.fori_loop(0, CHIP_ATOMS, clear_rows, 0, unroll=8)

    def half_group(rr, core):
        return modes.at[:, :, core, :, lanes_of(rr)]

    def forward_copy(rr):
        return remote(half_group(rr, s), half_group(rr, s), fwd_send.at[rr], fwd_recv.at[rr], sib)

    def build(rr, core):
        for e in range(3):
            for xh in range(2):
                v = modes[e, 4 * xh : 4 * xh + 4, core, :, lanes_of(rr)]
                vt = v.reshape(LANE, LANE).astype(F32).T
                for g in range(16):
                    at = rr * 32 + (g // 4) * 256 + (g % 4) * 8
                    wide[pl.ds(at, 8), e * 4 + xh + 2 * core, :] = vt[g * 8 : g * 8 + 8]

    def arrive(i, carry):
        rr = lax.rem(r + 7 - i, 8)

        def wait_one(cc, carry):
            ks = rr * 8 + cc

            @pl.when(ks != me)
            def _():
                chunk = modes.at[:, cc, s, :, lanes_of(rr)]
                remote(chunk, chunk, panel_send.at[0], panel_recv.at[ks], sib).wait_recv()

            return carry

        lax.fori_loop(0, 8, wait_one, 0)
        forward_copy(rr).start()
        build(rr, s)
        return carry

    lax.fori_loop(0, 8, arrive, 0)

    index_copy(0, 0).start()
    index_copy(1, 1).start()

    down = lax.broadcasted_iota(jnp.int32, (48, LANE), 0)
    across = lax.broadcasted_iota(jnp.int32, (48, LANE), 1)
    six = lax.rem(down, 6)
    place48 = (down // 6) * 16 + (six // 2) * 4 + lax.rem(six, 2) + 2 * s
    shut = jnp.where(place48 == across, 1.0, 0.0).astype(BF16)
    down = lax.broadcasted_iota(jnp.int32, (LANE, 96), 0)
    across = lax.broadcasted_iota(jnp.int32, (LANE, 96), 1)
    six = lax.rem(across, 6)
    core_at = jnp.where(across < 48, s, 1 - s)
    place96 = (lax.rem(across, 48) // 6) * 16 + (six // 2) * 4 + lax.rem(six, 2) + 2 * core_at
    open_up = jnp.where(place96 == down, 1.0, 0.0).astype(BF16)

    def pack_rows(atoms):
        rows = [wide[at] for at in atoms]
        stacked = jnp.concatenate(rows, axis=0).astype(BF16)
        return jnp.dot(shut, stacked, preferred_element_type=F32).astype(BF16)

    nxt = chip_device(lax.rem(me + 1, CHIPS))
    prv = chip_device(lax.rem(me + CHIPS - 1, CHIPS))

    def ghost_copy_of(n, h):
        piece = pl.ds(h * 8, 8)
        return remote(
            (to_next, to_prev)[n].at[piece], gin.at[n, s, piece],
            ghost_send_sem.at[n, h], ghost_recv_sem.at[n, h], (nxt, prv)[n],
        )

    def share_copy_of(n, h, half):
        piece = gin.at[n, half, pl.ds(h * 8, 8)]
        return remote(piece, piece, gfwd_send.at[n, h], gfwd_recv.at[n, h], sib)

    pieces = [(n, h) for h in range(2) for n in range(2)]

    def pick(g, carry):
        to_next[g] = pack_rows([n0 + ghost_s[1, 0, g * 8 + u] for u in range(8)])
        to_prev[g] = pack_rows([ghost_s[0, 1, g * 8 + u] for u in range(8)])
        return carry

    for h in range(2):
        lax.fori_loop(h * 8, h * 8 + 8, pick, 0, unroll=4)
        for n in range(2):
            ghost_copy_of(n, h).start()

    def finish(rr, carry):
        other = half_group(rr, 1 - s)
        remote(other, other, fwd_send.at[rr], fwd_recv.at[rr], sib).wait_recv()
        build(rr, 1 - s)
        for b in range(4):
            first_atom = pl.multiple_of(b * 256 + rr * 32, 32)
            table[pl.ds(first_atom, 32)] = wide[pl.ds(first_atom, 32)].astype(BF16)
        return carry

    lax.fori_loop(0, 8, finish, 0)

    def pick_own(g, carry):
        table[OWN_AFTER + g] = table[n0 + ghost_s[1, 1, g]]
        table[OWN_BEFORE + g] = table[ghost_s[0, 0, g]]
        return carry

    lax.fori_loop(0, GHOST, pick_own, 0, unroll=8)

    def unpack(n, h):
        base = (FROM_PREV, FROM_NEXT)[n] + h * 64

        def step(g, carry):
            both = jnp.concatenate([gin[n, s, h * 8 + g], gin[n, 1 - s, h * 8 + g]], axis=0)
            rows = jnp.dot(open_up, both, preferred_element_type=F32)
            table[pl.ds(base + g * 8, 8)] = rows.astype(BF16).reshape(8, 16, LANE)
            return carry

        lax.fori_loop(0, 8, step, 0, unroll=4)

    for n, h in pieces:
        ghost_copy_of(n, h).wait_recv()
        share_copy_of(n, h, s).start()
    for n, h in pieces:
        share_copy_of(n, h, 1 - s).wait_recv()
        unpack(n, h)

    def pull(n, idx_s):
        i0 = n * UNROLL
        b = i0 // LANE
        t0 = lax.rem(i0, LANE)
        q0 = (t0 // 32) * LANE + b * 32 + lax.rem(t0, 32)
        taken = [
            jnp.concatenate([table[idx_s[u, j]] for j in range(NBR)], axis=0)
            for u in range(UNROLL)
        ]
        sums = [
            jnp.dot(weights[i0 + u], taken[u], preferred_element_type=F32) for u in range(UNROLL)
        ]
        for u in range(UNROLL):
            for g in range(5):
                total = sums[u][g * 8 : g * 8 + 8] + sums[u][40 + g * 8 : 48 + g * 8]
                pulled[pl.ds(g * 8 * PITCH + q0 + u, 8, stride=PITCH), :] = total

    def pull_two(n, carry):
        for slot, indices in enumerate((idx_a, idx_b)):
            index_copy(2 * n + slot, slot).wait()
            pull(2 * n + slot, indices)

            @pl.when(n + 1 < HALF // UNROLL // 2)
            def _():
                index_copy(2 * n + 2 + slot, slot).start()

        return carry

    lax.fori_loop(0, HALF // UNROLL // 2, pull_two, 0)

    where = {"x": x, "y": y, "z": z}
    orders = ("xyz", "yzx", "zxy")

    def device_at(axis, j):
        if axis == "x":
            return (r, (j * 2 + zl) * 2 + s)
        if axis == "y":
            return (zh * 4 + j, c)
        return ((j // 2) * 4 + y, (x * 2 + lax.rem(j, 2)) * 2 + s)

    my_lanes = pl.ds(pl.multiple_of(s * HALF, HALF), HALF)

    lane_group = lax.broadcasted_iota(jnp.int32, (16, LANE), 1) // 32
    low = lane_group < 2
    even = lax.rem(lane_group, 2) == 0

    def velocity(a, core, keep):
        def part(zz, carry):
            rows = [
                pl.ds(pl.multiple_of(((a * 3 + comp) * 4 + 2 * core + xx) * PITCH, 8), HALF)
                for comp in range(3)
                for xx in range(2)
            ]
            rhs = jnp.concatenate(
                [
                    jnp.concatenate([pulled[rows[2 * comp], :], pulled[rows[2 * comp + 1], :]], axis=1)
                    for comp in range(3)
                ],
                axis=0,
            ).astype(BF16)
            lhs = jnp.concatenate(
                [
                    modes[comp, pl.ds(zz * 4, 4), :, :, my_lanes].reshape(256, HALF)
                    for comp in range(3)
                ],
                axis=1,
            )
            acc = jnp.dot(lhs, rhs, preferred_element_type=F32)
            for yy in range(4):
                for xx in range(2):
                    at = yy * 64
                    rows = [
                        acc[at + 16 * g : at + 16 * g + 16, xx * LANE : xx * LANE + LANE]
                        for g in range(4)
                    ]
                    halves = [None] * 4
                    for g in range(2):
                        halves[g] = jnp.where(low, rows[g], pltpu.roll(rows[g + 2], 64, 1))
                        halves[g + 2] = jnp.where(low, pltpu.roll(rows[g], 64, 1), rows[g + 2])
                    quarters = [None] * 4
                    for g in (0, 2):
                        quarters[g] = jnp.where(even, halves[g], pltpu.roll(halves[g + 1], 32, 1))
                        quarters[g + 1] = jnp.where(even, pltpu.roll(halves[g], 96, 1), halves[g + 1])
                    for quarter, block in enumerate(quarters):
                        xl, ll = divmod(quarter, 2)
                        pos = {"x": 2 * xx + xl, "y": yy, "z": 2 * zz + ll}
                        p, q, t = (pos[axis] for axis in orders[a])
                        place = (p * 4 + q) * 4 + t
                        if keep:
                            vkeep[a, place] = block
                        else:
                            vsend[a, place] = block.astype(BF16)
            return carry

        lax.fori_loop(0, 2, part, 0)

    def core_copy(a):
        return remote(vsend.at[a], vrecv.at[a], core_send.at[a], core_recv.at[a], sib)

    def stage_copies(a, stage, src, dst, ssem, rsem, size):
        axis = orders[a][stage]
        mine = where[axis]
        copies = []
        for d in range(1, 4):
            j = lax.rem(mine + d, 4)
            copies.append(
                remote(
                    src.at[a, pl.ds(j * size, size)], dst.at[a, mine],
                    ssem.at[a, d - 1], rsem.at[a, mine], device_at(axis, j),
                )
            )
        return copies

    def stage_wait(a, stage, dst, rsem):
        axis = orders[a][stage]
        mine = where[axis]
        total = None
        for d in range(1, 4):
            j = lax.rem(mine + d, 4)
            remote(dst.at[a, j], dst.at[a, j], rsem.at[a, j], rsem.at[a, j], sib).wait_recv()
            term = dst[a, j].astype(F32)
            total = term if total is None else total + term
        return total

    def copies1(a):
        return stage_copies(a, 0, send1, recv1, s1_send, s1_recv, 16)

    def copies2(a):
        return stage_copies(a, 1, part2, recv2, s2_send, s2_recv, 4)

    def copies3(a):
        return stage_copies(a, 2, part3, recv3, s3_send, s3_recv, 1)

    def add1(a):
        core_copy(a).wait_recv()

        def step(n, carry):
            at = pl.ds(n * 8, 8)
            both = vkeep[a, at] + vrecv[a, at].astype(F32)
            part1[a, at] = both
            send1[a, at] = both.astype(BF16)
            return carry

        lax.fori_loop(0, 8, step, 0)
        for copy in copies1(a):
            copy.start()

    def add2(a):
        mine = where[orders[a][0]]
        total = part1[a, pl.ds(mine * 16, 16)] + stage_wait(a, 0, recv1, s1_recv)
        part2[a] = total
        for copy in copies2(a):
            copy.start()

    def add3(a):
        mine = where[orders[a][1]]
        total = part2[a, pl.ds(mine * 4, 4)] + stage_wait(a, 1, recv2, s2_recv)
        part3[a] = total
        for copy in copies3(a):
            copy.start()

    def add4(a):
        mine = where[orders[a][2]]
        total = part3[a, pl.ds(mine, 1)] + stage_wait(a, 2, recv3, s3_recv)
        turned = jnp.concatenate([total[0], jnp.zeros((LANE - 16, LANE), F32)], axis=0).T
        out[a] = jnp.concatenate([turned[g * 32 : g * 32 + 32, :16] for g in range(4)], axis=1)

    for a in range(3):
        velocity(a, 1 - s, False)
        core_copy(a).start()
        if a:
            add1(a - 1)
        velocity(a, s, True)
    add1(2)
    for a in range(3):
        add2(a)
    for a in range(3):
        add3(a)
    for a in range(3):
        add4(a)

    def panel_done(i, carry):
        panel_copy(i).wait_send()
        return carry

    lax.fori_loop(1, CHIPS, panel_done, 0)

    def forward_done(i, carry):
        forward_copy(i).wait_send()
        return carry

    lax.fori_loop(0, 8, forward_done, 0)
    for n, h in pieces:
        ghost_copy_of(n, h).wait_send()
        share_copy_of(n, h, s).wait_send()
    for a in range(3):
        core_copy(a).wait_send()
        for copy in copies1(a) + copies2(a) + copies3(a):
            copy.wait_send()


def body(mode_panel, domain_sizes, ghost_send, neighbours, force_blocks, bond_vectors):
    panel = mode_panel.transpose(1, 2, 0, 3).reshape(3, 32, 8192)
    any_spec = pl.BlockSpec(memory_space=pl.ANY)
    vm = pltpu.VMEM
    dma = pltpu.SemaphoreType.DMA
    turned = pl.pallas_call(
        kernel,
        out_shape=jax.ShapeDtypeStruct((3, 32, 64), F32),
        in_specs=[any_spec, pl.BlockSpec(memory_space=pltpu.SMEM)] + [any_spec] * 4,
        out_specs=pl.BlockSpec(memory_space=vm),
        scratch_shapes=[
            vm((3, 8, 2, 32, CHIP_ATOMS), BF16),
            vm((TABLE, 16, LANE), BF16),
            vm((CHIP_ATOMS, 16, LANE), F32),
            vm((2, 144, CAP), F32),
            vm((2, 48, CAP), F32),
            vm((2, NBR, CAP), jnp.int32),
            vm((2, 2, GHOST), jnp.int32),
            vm((192, CHIP_ATOMS), F32),
            vm((NBR, CHIP_ATOMS), jnp.int32),
            vm((HALF, LANE), jnp.int32),
            pltpu.SMEM((UNROLL, LANE), jnp.int32),
            pltpu.SMEM((UNROLL, LANE), jnp.int32),
            pltpu.SMEM((2, 2, GHOST), jnp.int32),
            vm((256, LANE), F32),
            vm((HALF, 2 * WROWS, 256), BF16),
            vm((40 * PITCH, LANE), F32),
            vm((16, 48, LANE), BF16),
            vm((16, 48, LANE), BF16),
            vm((2, 2, 16, 48, LANE), BF16),
            vm((3, 64, 16, LANE), F32),
            vm((3, 64, 16, LANE), BF16),
            vm((3, 64, 16, LANE), BF16),
            vm((3, 64, 16, LANE), F32),
            vm((3, 64, 16, LANE), BF16),
            vm((3, 4, 16, 16, LANE), BF16),
            vm((3, 16, 16, LANE), F32),
            vm((3, 4, 4, 16, LANE), F32),
            vm((3, 4, 16, LANE), F32),
            vm((3, 4, 1, 16, LANE), F32),
            dma((5,)), dma((4,)), dma((4,)), dma((CHIPS,)), dma((CHIPS,)), dma((CHIPS,)), dma((CHIPS,)),
            dma((2, 2)), dma((2, 2)), dma((2, 2)), dma((2, 2)),
            dma((3,)), dma((3,)),
            dma((3, 3)), dma((3, 4)), dma((3, 3)), dma((3, 4)), dma((3, 3)), dma((3, 4)),
        ],
        compiler_params=pltpu.CompilerParams(
            collective_id=1, has_side_effects=True, vmem_limit_bytes=63 * 2**20
        ),
    )(
        panel,
        domain_sizes,
        ghost_send.reshape(2, 128),
        neighbours.reshape(16, 768),
        force_blocks.reshape(144, 768),
        bond_vectors.reshape(48, 768),
    )
    return turned.transpose(0, 2, 1)


def solution(mesh):
    return jax.shard_map(
        body,
        mesh=mesh,
        in_specs=(
            P("col", None, "row", None),
            P(),
            P(("row", "col"), None, None),
            P(("row", "col"), None, None),
            P(("row", "col"), None, None, None, None),
            P(("row", "col"), None, None, None),
        ),
        out_specs=P(None, "row", "col"),
        check_vma=False,
    )
```

```python
import jax
import jax.numpy as jnp
from jax import lax
from jax.experimental import pallas as pl
from jax.experimental.pallas import tpu as pltpu
from jax.sharding import PartitionSpec as P

MESH = pl.DeviceIdType.MESH
BF16 = jnp.bfloat16
F32 = jnp.float32

CHIPS = 64
CAP = 768
CHIP_ATOMS = 1024
HALF = 512
NBR = 16
GHOST = 128
LANE = 128
WROWS = 40
PITCH = 520
WHALF = LANE * WROWS
UNROLL = 32
STEP = 5
FROM_PREV = 1024
OWN_AFTER = 1152
OWN_BEFORE = 1280
FROM_NEXT = 1408
ZERO_ROW = 1536
TABLE = 1544


def kernel(
    panel, sizes, ghosts, nbrs, force, bond, out,
    modes, table, wide, raw_f, raw_b, raw_n, raw_g, merged, merged_n,
    idx_v, idx_a, idx_b, ghost_s, u32, weights, pulled, to_next, to_prev, gin,
    vkeep, vsend, vrecv, part1, send1, recv1, part2, recv2,
    local_sem, raw_send, raw_recv, panel_send, panel_recv, fwd_send, fwd_recv,
    ghost_send_sem, ghost_recv_sem, gfwd_send, gfwd_recv,
    core_send, core_recv, s1_send, s1_recv, s2_send, s2_recv,
):
    r = lax.axis_index("row")
    c = lax.axis_index("col")
    s = lax.rem(c, 2)
    cp = c // 2
    me = r * 8 + cp
    zh, y = r // 4, lax.rem(r, 4)
    x, zl = cp // 2, lax.rem(cp, 2)
    z = zh * 2 + zl
    sib = (r, cp * 2 + 1 - s)

    def chip_device(k):
        return (k // 8, lax.rem(k, 8) * 2 + s)

    def lanes_of(k):
        return pl.ds(pl.multiple_of(k * LANE, LANE), LANE)

    def remote(src, dst, ssem, rsem, dev):
        return pltpu.make_async_remote_copy(
            src_ref=src, dst_ref=dst, send_sem=ssem, recv_sem=rsem,
            device_id=dev, device_id_type=MESH,
        )

    barrier = pltpu.get_barrier_semaphore()
    pl.semaphore_signal(barrier, inc=1, device_id=sib, device_id_type=MESH)

    def greet(i, carry):
        k = lax.rem(me + i, CHIPS)
        pl.semaphore_signal(barrier, inc=1, device_id=chip_device(k), device_id_type=MESH)
        return carry

    lax.fori_loop(1, CHIPS, greet, 0, unroll=9)

    raws = ((force, raw_f), (bond, raw_b), (nbrs, raw_n), (ghosts, raw_g))
    own = [
        pltpu.make_async_copy(src, dst.at[s], local_sem.at[n])
        for n, (src, dst) in enumerate(raws)
    ]
    own.append(
        pltpu.make_async_copy(
            panel.at[:, :, lanes_of(me)], modes.at[:, cp, s, :, lanes_of(r)], local_sem.at[4]
        )
    )
    for copy in own:
        copy.start()
    pl.semaphore_wait(barrier, CHIPS)

    raw_copies = [
        remote(src, dst.at[s], raw_send.at[n], raw_recv.at[n], sib)
        for n, (src, dst) in enumerate(raws)
    ]
    for copy in raw_copies:
        copy.start()

    def panel_copy(i):
        k = lax.rem(me + i * STEP, CHIPS)
        return remote(
            panel.at[:, :, lanes_of(k)], modes.at[:, cp, s, :, lanes_of(r)],
            panel_send.at[i], panel_recv.at[me], chip_device(k),
        )

    def panel_start(i, carry):
        panel_copy(i).start()
        return carry

    lax.fori_loop(1, CHIPS, panel_start, 0, unroll=7)
    zero8 = jnp.zeros((8, LANE), F32)

    def clear_w(i, carry):
        pulled[pl.ds(i * 8, 8), :] = zero8
        return carry

    lax.fori_loop(0, 2 * WHALF // 8, clear_w, 0)

    for i in range(32):
        u32[pl.ds(i * 8, 8), :] = zero8
    table[pl.ds(ZERO_ROW, TABLE - ZERO_ROW)] = jnp.zeros((TABLE - ZERO_ROW, 16, LANE), BF16)
    for copy in own:
        copy.wait()
    for copy in raw_copies:
        copy.wait()
    ghost_copy = pltpu.make_async_copy(raw_g, ghost_s, local_sem.at[0])
    ghost_copy.start()

    n0 = sizes[2 * me]
    lane = lax.broadcasted_iota(jnp.int32, (8, CHIP_ATOMS), 1)
    first = lane < n0

    def merge(x0, x1):
        pad = jnp.zeros((8, CHIP_ATOMS - CAP), x0.dtype)
        a = jnp.concatenate([x0, pad], axis=1)
        b = pltpu.roll(jnp.concatenate([x1, pad], axis=1), n0, 1)
        return jnp.where(first, a, b)

    def merge_force(g, carry):
        rows = pl.ds(pl.multiple_of(g * 8, 8), 8)
        merged[rows, :] = merge(raw_f[0, rows, :], raw_f[1, rows, :])
        return carry

    def merge_bond(g, carry):
        rows = pl.ds(pl.multiple_of(g * 8, 8), 8)
        merged[pl.ds(pl.multiple_of(144 + g * 8, 8), 8), :] = merge(
            raw_b[0, rows, :], raw_b[1, rows, :]
        )
        return carry

    lax.fori_loop(0, 18, merge_force, 0)
    lax.fori_loop(0, 6, merge_bond, 0)
    for g in range(2):
        rows = pl.ds(g * 8, 8)
        merged_n[rows, :] = merge(raw_n[0, rows, :], raw_n[1, rows, :])
    for b in range(4):
        v = merged_n[:, lanes_of(2 * b + s)]
        pos = (2 * b + s) * LANE + lax.broadcasted_iota(jnp.int32, (NBR, LANE), 1)
        late = pos >= n0
        inner = v + jnp.where(late, n0, 0)
        outer = v + jnp.where(late, 512, 256)
        row = jnp.where(v < CAP, inner, jnp.where(v >= CHIP_ATOMS, ZERO_ROW, outer))
        square = jnp.concatenate([row, jnp.zeros((LANE - NBR, LANE), jnp.int32)], axis=0)
        idx_v[pl.ds(b * LANE, LANE), :] = square.T

    block_lane = lax.rem(lax.broadcasted_iota(jnp.int32, (LANE, LANE), 1), 4)

    def weights_block(b, carry):
        tile = lanes_of(2 * b + s)

        def one(ac, carry):
            a = ac // 3
            comp = lax.rem(ac, 3)
            bv = merged[pl.ds(pl.multiple_of(144 + a * 16, 16), 16), tile]
            for e in range(3):
                w = bv * merged[pl.ds(pl.multiple_of((comp * 3 + e) * 16, 16), 16), tile]
                for m in range(4):
                    for half in range(2):
                        u32[pl.ds(half * 128 + e * 4 + m, 8, stride=16), :] = w[half * 8 : half * 8 + 8]
            for half in range(2):
                t = u32[pl.ds(half * 128, 128), :].T
                for m in range(4):
                    tm = jnp.where(block_lane == m, t, 0.0)
                    for g in range(16):
                        pulled[pl.ds(half * WHALF + g * 8 * WROWS + ac * 4 + m, 8, stride=WROWS), :] = tm[g * 8 : g * 8 + 8]
            return carry

        lax.fori_loop(0, 9, one, 0)

        def pack(t, carry):
            for half in range(2):
                w = pulled[pl.ds(pl.multiple_of(half * WHALF + t * WROWS, 8), WROWS), :]
                high = w.astype(BF16).astype(F32)
                both = jnp.concatenate([high, w - high], axis=0).astype(BF16)
                weights[b * LANE + t, :, half * LANE : half * LANE + LANE] = both
            return carry

        lax.fori_loop(0, LANE, pack, 0, unroll=4)
        return carry

    lax.fori_loop(0, 4, weights_block, 0)
    ghost_copy.wait()

    def index_copy(n, slot):
        return pltpu.make_async_copy(
            idx_v.at[pl.ds(pl.multiple_of(n * UNROLL, UNROLL), UNROLL)],
            (idx_a, idx_b)[slot], local_sem.at[slot],
        )

    def clear_rows(i, carry):
        wide[i, pl.ds(12, 4), :] = jnp.zeros((4, LANE), F32)
        return carry

    lax.fori_loop(0, CHIP_ATOMS, clear_rows, 0, unroll=8)

    def half_group(rr, core):
        return modes.at[:, :, core, :, lanes_of(rr)]

    def forward_copy(rr):
        return remote(half_group(rr, s), half_group(rr, s), fwd_send.at[rr], fwd_recv.at[rr], sib)

    def build(rr, core):
        for e in range(3):
            for xh in range(2):
                v = modes[e, 4 * xh : 4 * xh + 4, core, :, lanes_of(rr)]
                vt = v.reshape(LANE, LANE).astype(F32).T
                for g in range(16):
                    at = rr * 32 + (g // 4) * 256 + (g % 4) * 8
                    wide[pl.ds(at, 8), e * 4 + xh + 2 * core, :] = vt[g * 8 : g * 8 + 8]

    def arrive(i, carry):
        rr = lax.rem(r + 7 - i, 8)

        def wait_one(cc, carry):
            ks = rr * 8 + cc

            @pl.when(ks != me)
            def _():
                chunk = modes.at[:, cc, s, :, lanes_of(rr)]
                remote(chunk, chunk, panel_send.at[0], panel_recv.at[ks], sib).wait_recv()

            return carry

        lax.fori_loop(0, 8, wait_one, 0)
        forward_copy(rr).start()
        build(rr, s)
        return carry

    lax.fori_loop(0, 8, arrive, 0)

    index_copy(0, 0).start()
    index_copy(1, 1).start()

    down = lax.broadcasted_iota(jnp.int32, (48, LANE), 0)
    across = lax.broadcasted_iota(jnp.int32, (48, LANE), 1)
    six = lax.rem(down, 6)
    place48 = (down // 6) * 16 + (six // 2) * 4 + lax.rem(six, 2) + 2 * s
    shut = jnp.where(place48 == across, 1.0, 0.0).astype(BF16)
    down = lax.broadcasted_iota(jnp.int32, (LANE, 96), 0)
    across = lax.broadcasted_iota(jnp.int32, (LANE, 96), 1)
    six = lax.rem(across, 6)
    core_at = jnp.where(across < 48, s, 1 - s)
    place96 = (lax.rem(across, 48) // 6) * 16 + (six // 2) * 4 + lax.rem(six, 2) + 2 * core_at
    open_up = jnp.where(place96 == down, 1.0, 0.0).astype(BF16)

    def pack_rows(atoms):
        rows = [wide[at] for at in atoms]
        stacked = jnp.concatenate(rows, axis=0).astype(BF16)
        return jnp.dot(shut, stacked, preferred_element_type=F32).astype(BF16)

    nxt = chip_device(lax.rem(me + 1, CHIPS))
    prv = chip_device(lax.rem(me + CHIPS - 1, CHIPS))

    def ghost_copy_of(n, h):
        piece = pl.ds(h * 8, 8)
        return remote(
            (to_next, to_prev)[n].at[piece], gin.at[n, s, piece],
            ghost_send_sem.at[n, h], ghost_recv_sem.at[n, h], (nxt, prv)[n],
        )

    def share_copy_of(n, h, half):
        piece = gin.at[n, half, pl.ds(h * 8, 8)]
        return remote(piece, piece, gfwd_send.at[n, h], gfwd_recv.at[n, h], sib)

    pieces = [(n, h) for h in range(2) for n in range(2)]

    def pick(g, carry):
        to_next[g] = pack_rows([n0 + ghost_s[1, 0, g * 8 + u] for u in range(8)])
        to_prev[g] = pack_rows([ghost_s[0, 1, g * 8 + u] for u in range(8)])
        return carry

    for h in range(2):
        lax.fori_loop(h * 8, h * 8 + 8, pick, 0, unroll=4)
        for n in range(2):
            ghost_copy_of(n, h).start()

    def finish(rr, carry):
        other = half_group(rr, 1 - s)
        remote(other, other, fwd_send.at[rr], fwd_recv.at[rr], sib).wait_recv()
        build(rr, 1 - s)
        for b in range(4):
            first_atom = pl.multiple_of(b * 256 + rr * 32, 32)
            table[pl.ds(first_atom, 32)] = wide[pl.ds(first_atom, 32)].astype(BF16)
        return carry

    lax.fori_loop(0, 8, finish, 0)

    def pick_own(g, carry):
        table[OWN_AFTER + g] = table[n0 + ghost_s[1, 1, g]]
        table[OWN_BEFORE + g] = table[ghost_s[0, 0, g]]
        return carry

    lax.fori_loop(0, GHOST, pick_own, 0, unroll=8)

    def unpack(n, h):
        base = (FROM_PREV, FROM_NEXT)[n] + h * 64

        def step(g, carry):
            both = jnp.concatenate([gin[n, s, h * 8 + g], gin[n, 1 - s, h * 8 + g]], axis=0)
            rows = jnp.dot(open_up, both, preferred_element_type=F32)
            table[pl.ds(base + g * 8, 8)] = rows.astype(BF16).reshape(8, 16, LANE)
            return carry

        lax.fori_loop(0, 8, step, 0, unroll=4)

    def panel_done(i, carry):
        panel_copy(i).wait_send()
        return carry

    lax.fori_loop(1, CHIPS, panel_done, 0, unroll=7)

    def forward_done(i, carry):
        forward_copy(i).wait_send()
        return carry

    lax.fori_loop(0, 8, forward_done, 0)
    for n, h in pieces:
        ghost_copy_of(n, h).wait_recv()
        share_copy_of(n, h, s).start()
    for n, h in pieces:
        share_copy_of(n, h, 1 - s).wait_recv()
        unpack(n, h)

    def pull(n, idx_s):
        i0 = n * UNROLL
        b = i0 // LANE
        t0 = lax.rem(i0, LANE)
        q0 = (t0 // 32) * LANE + b * 32 + lax.rem(t0, 32)
        taken = [
            jnp.concatenate([table[idx_s[u, j]] for j in range(NBR)], axis=0)
            for u in range(UNROLL)
        ]
        sums = [
            jnp.dot(weights[i0 + u], taken[u], preferred_element_type=F32) for u in range(UNROLL)
        ]
        for u in range(UNROLL):
            for g in range(5):
                total = sums[u][g * 8 : g * 8 + 8] + sums[u][40 + g * 8 : 48 + g * 8]
                pulled[pl.ds(g * 8 * PITCH + q0 + u, 8, stride=PITCH), :] = total

    def pull_two(n, carry):
        for slot, indices in enumerate((idx_a, idx_b)):
            index_copy(2 * n + slot, slot).wait()
            pull(2 * n + slot, indices)

            @pl.when(n + 1 < HALF // UNROLL // 2)
            def _():
                index_copy(2 * n + 2 + slot, slot).start()

        return carry

    lax.fori_loop(0, HALF // UNROLL // 2, pull_two, 0)

    where = {"x": x, "y": y, "z": z}
    orders = ("xyz", "yzx", "zxy")

    def device_at(axis, j):
        if axis == "x":
            return (r, (j * 2 + zl) * 2 + s)
        if axis == "y":
            return (zh * 4 + j, c)
        return ((j // 2) * 4 + y, (x * 2 + lax.rem(j, 2)) * 2 + s)

    my_lanes = pl.ds(pl.multiple_of(s * HALF, HALF), HALF)

    lane_group = lax.broadcasted_iota(jnp.int32, (16, LANE), 1) // 32
    low = lane_group < 2
    even = lax.rem(lane_group, 2) == 0

    def velocity(a, core, keep):
        def part(zz, carry):
            rows = [
                pl.ds(pl.multiple_of(((a * 3 + comp) * 4 + 2 * core + xx) * PITCH, 8), HALF)
                for comp in range(3)
                for xx in range(2)
            ]
            rhs = jnp.concatenate(
                [
                    jnp.concatenate([pulled[rows[2 * comp], :], pulled[rows[2 * comp + 1], :]], axis=1)
                    for comp in range(3)
                ],
                axis=0,
            ).astype(BF16)
            lhs = jnp.concatenate(
                [
                    modes[comp, :, :, :, my_lanes].reshape(HALF, HALF)
                    for comp in range(3)
                ],
                axis=1,
            )
            acc = jnp.dot(lhs, rhs, preferred_element_type=F32)
            for zz, yy, xx in [(i // 8, i // 2 % 4, i % 2) for i in range(16)]:
                    at = zz * 256 + yy * 64
                    rows = [
                        acc[at + 16 * g : at + 16 * g + 16, xx * LANE : xx * LANE + LANE]
                        for g in range(4)
                    ]
                    halves = [None] * 4
                    for g in range(2):
                        halves[g] = jnp.where(low, rows[g], pltpu.roll(rows[g + 2], 64, 1))
                        halves[g + 2] = jnp.where(low, pltpu.roll(rows[g], 64, 1), rows[g + 2])
                    quarters = [None] * 4
                    for g in (0, 2):
                        quarters[g] = jnp.where(even, halves[g], pltpu.roll(halves[g + 1], 32, 1))
                        quarters[g + 1] = jnp.where(even, pltpu.roll(halves[g], 96, 1), halves[g + 1])
                    for quarter, block in enumerate(quarters):
                        xl, ll = divmod(quarter, 2)
                        pos = {"x": 2 * xx + xl, "y": yy, "z": 2 * zz + ll}
                        p, q, t = (pos[axis] for axis in orders[a])
                        place = (p * 4 + q) * 4 + t
                        if keep:
                            vkeep[a, place] = block
                        else:
                            vsend[a, place] = block.astype(BF16)
            return carry

        lax.fori_loop(0, 1, part, 0)

    def core_copy(a):
        return remote(vsend.at[a], vrecv.at[a], core_send.at[a], core_recv.at[a], sib)

    def stage_copies(a, stage, src, dst, ssem, rsem, size):
        axis = orders[a][stage]
        mine = where[axis]
        copies = []
        for d in range(1, 4):
            j = lax.rem(mine + d, 4)
            copies.append(
                remote(
                    src.at[a, pl.ds(j * size, size)], dst.at[a, mine],
                    ssem.at[a, d - 1], rsem.at[a, mine], device_at(axis, j),
                )
            )
        return copies

    def stage_wait(a, stage, dst, rsem):
        axis = orders[a][stage]
        mine = where[axis]
        total = None
        for d in range(1, 4):
            j = lax.rem(mine + d, 4)
            remote(dst.at[a, j], dst.at[a, j], rsem.at[a, j], rsem.at[a, j], sib).wait_recv()
            term = dst[a, j].astype(F32)
            total = term if total is None else total + term
        return total

    def copies1(a):
        return stage_copies(a, 0, send1, recv1, s1_send, s1_recv, 16)

    def plane_copy(a, d):
        first_axis, second_axis = orders[a][1:]
        mine = where[first_axis] * 4 + where[second_axis]
        other = lax.rem(mine + d, 16)
        at = dict(where)
        at[first_axis] = other // 4
        at[second_axis] = lax.rem(other, 4)
        dev = ((at["z"] // 2) * 4 + at["y"], (at["x"] * 2 + lax.rem(at["z"], 2)) * 2 + s)
        out_copy = remote(
            part2.at[a, other], recv2.at[a, mine], s2_send.at[a, d], s2_recv.at[a, mine], dev
        )
        return out_copy, other

    def plane_wait(a, other):
        piece = recv2.at[a, other]
        remote(piece, piece, s2_send.at[a, 0], s2_recv.at[a, other], sib).wait_recv()

    def add1(a):
        core_copy(a).wait_recv()

        def step(n, carry):
            at = pl.ds(n * 8, 8)
            both = vkeep[a, at] + vrecv[a, at].astype(F32)
            part1[a, at] = both
            send1[a, at] = both.astype(BF16)
            return carry

        lax.fori_loop(0, 8, step, 0)
        for copy in copies1(a):
            copy.start()

    def add2(a):
        mine = where[orders[a][0]]
        total = part1[a, pl.ds(mine * 16, 16)] + stage_wait(a, 0, recv1, s1_recv)
        part2[a] = total

        def send_one(d, carry):
            plane_copy(a, d)[0].start()
            return carry

        lax.fori_loop(1, 16, send_one, 0, unroll=5)

    def add3(a):
        mine = where[orders[a][1]] * 4 + where[orders[a][2]]

        def take_one(d, total):
            other = lax.rem(mine + d, 16)
            plane_wait(a, other)
            return total + recv2[a, other]

        total = lax.fori_loop(1, 16, take_one, part2[a, mine], unroll=5)
        turned = jnp.concatenate([total, jnp.zeros((LANE - 16, LANE), F32)], axis=0).T
        out[a] = jnp.concatenate([turned[g * 32 : g * 32 + 32, :16] for g in range(4)], axis=1)

    for a in range(3):
        velocity(a, 1 - s, False)
        core_copy(a).start()
        if a:
            add1(a - 1)
        velocity(a, s, True)
    add1(2)
    for a in range(3):
        add2(a)
    for n, h in pieces:
        ghost_copy_of(n, h).wait_send()
        share_copy_of(n, h, s).wait_send()
    for a in range(3):
        core_copy(a).wait_send()
        for copy in copies1(a):
            copy.wait_send()
    for a in range(3):
        add3(a)

    for a in range(3):

        def sent_one(d, carry, a=a):
            plane_copy(a, d)[0].wait_send()
            return carry

        lax.fori_loop(1, 16, sent_one, 0, unroll=5)


def body(mode_panel, domain_sizes, ghost_send, neighbours, force_blocks, bond_vectors):
    panel = mode_panel.transpose(1, 2, 0, 3).reshape(3, 32, 8192)
    any_spec = pl.BlockSpec(memory_space=pl.ANY)
    vm = pltpu.VMEM
    dma = pltpu.SemaphoreType.DMA
    turned = pl.pallas_call(
        kernel,
        out_shape=jax.ShapeDtypeStruct((3, 32, 64), F32),
        in_specs=[any_spec, pl.BlockSpec(memory_space=pltpu.SMEM)] + [any_spec] * 4,
        out_specs=pl.BlockSpec(memory_space=vm),
        scratch_shapes=[
            vm((3, 8, 2, 32, CHIP_ATOMS), BF16),
            vm((TABLE, 16, LANE), BF16),
            vm((CHIP_ATOMS, 16, LANE), F32),
            vm((2, 144, CAP), F32),
            vm((2, 48, CAP), F32),
            vm((2, NBR, CAP), jnp.int32),
            vm((2, 2, GHOST), jnp.int32),
            vm((192, CHIP_ATOMS), F32),
            vm((NBR, CHIP_ATOMS), jnp.int32),
            vm((HALF, LANE), jnp.int32),
            pltpu.SMEM((UNROLL, LANE), jnp.int32),
            pltpu.SMEM((UNROLL, LANE), jnp.int32),
            pltpu.SMEM((2, 2, GHOST), jnp.int32),
            vm((256, LANE), F32),
            vm((HALF, 2 * WROWS, 256), BF16),
            vm((40 * PITCH, LANE), F32),
            vm((16, 48, LANE), BF16),
            vm((16, 48, LANE), BF16),
            vm((2, 2, 16, 48, LANE), BF16),
            vm((3, 64, 16, LANE), F32),
            vm((3, 64, 16, LANE), BF16),
            vm((3, 64, 16, LANE), BF16),
            vm((3, 64, 16, LANE), F32),
            vm((3, 64, 16, LANE), BF16),
            vm((3, 4, 16, 16, LANE), BF16),
            vm((3, 16, 16, LANE), F32),
            vm((3, 16, 16, LANE), F32),
            dma((5,)), dma((4,)), dma((4,)), dma((CHIPS,)), dma((CHIPS,)), dma((CHIPS,)), dma((CHIPS,)),
            dma((2, 2)), dma((2, 2)), dma((2, 2)), dma((2, 2)),
            dma((3,)), dma((3,)),
            dma((3, 3)), dma((3, 4)), dma((3, 16)), dma((3, 16)),
        ],
        compiler_params=pltpu.CompilerParams(
            collective_id=1, has_side_effects=True, vmem_limit_bytes=63 * 2**20
        ),
    )(
        panel,
        domain_sizes,
        ghost_send.reshape(2, 128),
        neighbours.reshape(16, 768),
        force_blocks.reshape(144, 768),
        bond_vectors.reshape(48, 768),
    )
    return turned.transpose(0, 2, 1)


def solution(mesh):
    return jax.shard_map(
        body,
        mesh=mesh,
        in_specs=(
            P("col", None, "row", None),
            P(),
            P(("row", "col"), None, None),
            P(("row", "col"), None, None),
            P(("row", "col"), None, None, None, None),
            P(("row", "col"), None, None, None),
        ),
        out_specs=P(None, "row", "col"),
        check_vma=False,
    )
```

```python
import jax
import jax.numpy as jnp
from jax import lax
from jax.experimental import pallas as pl
from jax.experimental.pallas import tpu as pltpu
from jax.sharding import PartitionSpec as P

MESH = pl.DeviceIdType.MESH
BF16 = jnp.bfloat16
F32 = jnp.float32

CHIPS = 64
CAP = 768
CHIP_ATOMS = 1024
HALF = 512
NBR = 16
GHOST = 128
LANE = 128
WROWS = 40
PITCH = 520
WHALF = LANE * WROWS
UNROLL = 32
STEP = 5
FROM_PREV = 1024
OWN_AFTER = 1152
OWN_BEFORE = 1280
FROM_NEXT = 1408
ZERO_ROW = 1536
TABLE = 1544


def kernel(
    panel, sizes, ghosts, nbrs, force, bond, out,
    modes, table, wide, raw_f, raw_b, raw_n, raw_g, merged, merged_n,
    idx_v, idx_a, idx_b, ghost_s, u32, weights, pulled, to_next, to_prev, gin,
    vkeep, vsend, vrecv, part1, send1, recv1, part2, recv2,
    local_sem, raw_send, raw_recv, panel_send, panel_recv, fwd_send, fwd_recv,
    ghost_send_sem, ghost_recv_sem, gfwd_send, gfwd_recv,
    core_send, core_recv, s1_send, s1_recv, s2_send, s2_recv,
):
    r = lax.axis_index("row")
    c = lax.axis_index("col")
    s = lax.rem(c, 2)
    cp = c // 2
    me = r * 8 + cp
    zh, y = r // 4, lax.rem(r, 4)
    x, zl = cp // 2, lax.rem(cp, 2)
    z = zh * 2 + zl
    sib = (r, cp * 2 + 1 - s)

    def chip_device(k):
        return (k // 8, lax.rem(k, 8) * 2 + s)

    def lanes_of(k):
        return pl.ds(pl.multiple_of(k * LANE, LANE), LANE)

    def remote(src, dst, ssem, rsem, dev):
        return pltpu.make_async_remote_copy(
            src_ref=src, dst_ref=dst, send_sem=ssem, recv_sem=rsem,
            device_id=dev, device_id_type=MESH,
        )

    barrier = pltpu.get_barrier_semaphore()
    pl.semaphore_signal(barrier, inc=1, device_id=sib, device_id_type=MESH)

    def greet(i, carry):
        k = lax.rem(me + i, CHIPS)
        pl.semaphore_signal(barrier, inc=1, device_id=chip_device(k), device_id_type=MESH)
        return carry

    lax.fori_loop(1, CHIPS, greet, 0, unroll=9)

    raws = ((force, raw_f), (bond, raw_b), (nbrs, raw_n), (ghosts, raw_g))
    own = [
        pltpu.make_async_copy(src, dst.at[s], local_sem.at[n])
        for n, (src, dst) in enumerate(raws)
    ]
    own.append(
        pltpu.make_async_copy(
            panel.at[:, :, lanes_of(me)], modes.at[:, cp, s, :, lanes_of(r)], local_sem.at[4]
        )
    )
    for copy in own:
        copy.start()
    pl.semaphore_wait(barrier, CHIPS)

    raw_copies = [
        remote(src, dst.at[s], raw_send.at[n], raw_recv.at[n], sib)
        for n, (src, dst) in enumerate(raws)
    ]
    for copy in raw_copies:
        copy.start()

    def panel_copy(i):
        k = lax.rem(me + i * STEP, CHIPS)
        return remote(
            panel.at[:, :, lanes_of(k)], modes.at[:, cp, s, :, lanes_of(r)],
            panel_send.at[i], panel_recv.at[me], chip_device(k),
        )

    def panel_start(i, carry):
        panel_copy(i).start()
        return carry

    lax.fori_loop(1, CHIPS, panel_start, 0, unroll=7)
    zero8 = jnp.zeros((8, LANE), F32)

    def clear_w(i, carry):
        pulled[pl.ds(i * 8, 8), :] = zero8
        return carry

    lax.fori_loop(0, 2 * WHALF // 8, clear_w, 0)

    for i in range(32):
        u32[pl.ds(i * 8, 8), :] = zero8
    table[pl.ds(ZERO_ROW, TABLE - ZERO_ROW)] = jnp.zeros((TABLE - ZERO_ROW, 16, LANE), BF16)
    for copy in own:
        copy.wait()
    for copy in raw_copies:
        copy.wait()
    ghost_copy = pltpu.make_async_copy(raw_g, ghost_s, local_sem.at[0])
    ghost_copy.start()

    n0 = sizes[2 * me]
    lane = lax.broadcasted_iota(jnp.int32, (8, CHIP_ATOMS), 1)
    first = lane < n0

    def merge(x0, x1):
        pad = jnp.zeros((8, CHIP_ATOMS - CAP), x0.dtype)
        a = jnp.concatenate([x0, pad], axis=1)
        b = pltpu.roll(jnp.concatenate([x1, pad], axis=1), n0, 1)
        return jnp.where(first, a, b)

    def merge_force(g, carry):
        rows = pl.ds(pl.multiple_of(g * 8, 8), 8)
        merged[rows, :] = merge(raw_f[0, rows, :], raw_f[1, rows, :])
        return carry

    def merge_bond(g, carry):
        rows = pl.ds(pl.multiple_of(g * 8, 8), 8)
        merged[pl.ds(pl.multiple_of(144 + g * 8, 8), 8), :] = merge(
            raw_b[0, rows, :], raw_b[1, rows, :]
        )
        return carry

    lax.fori_loop(0, 18, merge_force, 0)
    lax.fori_loop(0, 6, merge_bond, 0)
    for g in range(2):
        rows = pl.ds(g * 8, 8)
        merged_n[rows, :] = merge(raw_n[0, rows, :], raw_n[1, rows, :])
    for b in range(4):
        v = merged_n[:, lanes_of(2 * b + s)]
        pos = (2 * b + s) * LANE + lax.broadcasted_iota(jnp.int32, (NBR, LANE), 1)
        late = pos >= n0
        inner = v + jnp.where(late, n0, 0)
        outer = v + jnp.where(late, 512, 256)
        row = jnp.where(v < CAP, inner, jnp.where(v >= CHIP_ATOMS, ZERO_ROW, outer))
        square = jnp.concatenate([row, jnp.zeros((LANE - NBR, LANE), jnp.int32)], axis=0)
        idx_v[pl.ds(b * LANE, LANE), :] = square.T

    block_lane = lax.rem(lax.broadcasted_iota(jnp.int32, (LANE, LANE), 1), 4)

    def weights_block(b, carry):
        tile = lanes_of(2 * b + s)

        def one(ac, carry):
            a = ac // 3
            comp = lax.rem(ac, 3)
            bv = merged[pl.ds(pl.multiple_of(144 + a * 16, 16), 16), tile]
            for e in range(3):
                w = bv * merged[pl.ds(pl.multiple_of((comp * 3 + e) * 16, 16), 16), tile]
                for m in range(4):
                    for half in range(2):
                        u32[pl.ds(half * 128 + e * 4 + m, 8, stride=16), :] = w[half * 8 : half * 8 + 8]
            for half in range(2):
                t = u32[pl.ds(half * 128, 128), :].T
                for m in range(4):
                    tm = jnp.where(block_lane == m, t, 0.0)
                    for g in range(16):
                        pulled[pl.ds(half * WHALF + g * 8 * WROWS + ac * 4 + m, 8, stride=WROWS), :] = tm[g * 8 : g * 8 + 8]
            return carry

        lax.fori_loop(0, 9, one, 0)

        def pack(t, carry):
            for half in range(2):
                w = pulled[pl.ds(pl.multiple_of(half * WHALF + t * WROWS, 8), WROWS), :]
                high = w.astype(BF16).astype(F32)
                both = jnp.concatenate([high, w - high], axis=0).astype(BF16)
                weights[b * LANE + t, :, half * LANE : half * LANE + LANE] = both
            return carry

        lax.fori_loop(0, LANE, pack, 0, unroll=4)
        return carry

    lax.fori_loop(0, 4, weights_block, 0)
    ghost_copy.wait()

    def index_copy(n, slot):
        return pltpu.make_async_copy(
            idx_v.at[pl.ds(pl.multiple_of(n * UNROLL, UNROLL), UNROLL)],
            (idx_a, idx_b)[slot], local_sem.at[slot],
        )

    def clear_rows(i, carry):
        wide[i, pl.ds(12, 4), :] = jnp.zeros((4, LANE), F32)
        return carry

    lax.fori_loop(0, CHIP_ATOMS, clear_rows, 0, unroll=8)

    def half_group(rr, core):
        return modes.at[:, :, core, :, lanes_of(rr)]

    def forward_copy(rr):
        return remote(half_group(rr, s), half_group(rr, s), fwd_send.at[rr], fwd_recv.at[rr], sib)

    def build(rr, core):
        for e in range(3):
            for xh in range(2):
                v = modes[e, 4 * xh : 4 * xh + 4, core, :, lanes_of(rr)]
                vt = v.reshape(LANE, LANE).astype(F32).T
                for g in range(16):
                    at = rr * 32 + (g // 4) * 256 + (g % 4) * 8
                    wide[pl.ds(at, 8), e * 4 + xh + 2 * core, :] = vt[g * 8 : g * 8 + 8]

    def arrive(i, carry):
        rr = lax.rem(r + 7 - i, 8)

        def wait_one(cc, carry):
            ks = rr * 8 + cc

            @pl.when(ks != me)
            def _():
                chunk = modes.at[:, cc, s, :, lanes_of(rr)]
                remote(chunk, chunk, panel_send.at[0], panel_recv.at[ks], sib).wait_recv()

            return carry

        lax.fori_loop(0, 8, wait_one, 0)
        build(rr, s)
        return carry

    lax.fori_loop(0, 8, arrive, 0)

    index_copy(0, 0).start()
    index_copy(1, 1).start()

    down = lax.broadcasted_iota(jnp.int32, (48, LANE), 0)
    across = lax.broadcasted_iota(jnp.int32, (48, LANE), 1)
    six = lax.rem(down, 6)
    place48 = (down // 6) * 16 + (six // 2) * 4 + lax.rem(six, 2) + 2 * s
    shut = jnp.where(place48 == across, 1.0, 0.0).astype(BF16)
    down = lax.broadcasted_iota(jnp.int32, (LANE, 96), 0)
    across = lax.broadcasted_iota(jnp.int32, (LANE, 96), 1)
    six = lax.rem(across, 6)
    core_at = jnp.where(across < 48, s, 1 - s)
    place96 = (lax.rem(across, 48) // 6) * 16 + (six // 2) * 4 + lax.rem(six, 2) + 2 * core_at
    open_up = jnp.where(place96 == down, 1.0, 0.0).astype(BF16)

    def pack_rows(atoms):
        rows = [wide[at] for at in atoms]
        stacked = jnp.concatenate(rows, axis=0).astype(BF16)
        return jnp.dot(shut, stacked, preferred_element_type=F32).astype(BF16)

    nxt = chip_device(lax.rem(me + 1, CHIPS))
    prv = chip_device(lax.rem(me + CHIPS - 1, CHIPS))

    def ghost_copy_of(n, h):
        piece = pl.ds(h * 8, 8)
        return remote(
            (to_next, to_prev)[n].at[piece], gin.at[n, s, piece],
            ghost_send_sem.at[n, h], ghost_recv_sem.at[n, h], (nxt, prv)[n],
        )

    def share_copy_of(n, h, half):
        piece = gin.at[n, half, pl.ds(h * 8, 8)]
        return remote(piece, piece, gfwd_send.at[n, h], gfwd_recv.at[n, h], sib)

    pieces = [(n, h) for h in range(2) for n in range(2)]

    def pick(g, carry):
        to_next[g] = pack_rows([n0 + ghost_s[1, 0, g * 8 + u] for u in range(8)])
        to_prev[g] = pack_rows([ghost_s[0, 1, g * 8 + u] for u in range(8)])
        return carry

    def forward(rr, carry):
        forward_copy(rr).start()
        return carry

    for h in range(2):
        lax.fori_loop(h * 8, h * 8 + 8, pick, 0, unroll=4)
        for n in range(2):
            ghost_copy_of(n, h).start()
        lax.fori_loop(h * 4, h * 4 + 4, forward, 0)

    def finish(rr, carry):
        other = half_group(rr, 1 - s)
        remote(other, other, fwd_send.at[rr], fwd_recv.at[rr], sib).wait_recv()
        build(rr, 1 - s)
        for b in range(4):
            first_atom = pl.multiple_of(b * 256 + rr * 32, 32)
            table[pl.ds(first_atom, 32)] = wide[pl.ds(first_atom, 32)].astype(BF16)
        return carry

    lax.fori_loop(0, 8, finish, 0)

    def pick_own(g, carry):
        table[OWN_AFTER + g] = table[n0 + ghost_s[1, 1, g]]
        table[OWN_BEFORE + g] = table[ghost_s[0, 0, g]]
        return carry

    lax.fori_loop(0, GHOST, pick_own, 0, unroll=8)

    def unpack(n, h):
        base = (FROM_PREV, FROM_NEXT)[n] + h * 64

        def step(g, carry):
            both = jnp.concatenate([gin[n, s, h * 8 + g], gin[n, 1 - s, h * 8 + g]], axis=0)
            rows = jnp.dot(open_up, both, preferred_element_type=F32)
            table[pl.ds(base + g * 8, 8)] = rows.astype(BF16).reshape(8, 16, LANE)
            return carry

        lax.fori_loop(0, 8, step, 0, unroll=4)

    def panel_done(i, carry):
        panel_copy(i).wait_send()
        return carry

    lax.fori_loop(1, CHIPS, panel_done, 0, unroll=7)

    def forward_done(i, carry):
        forward_copy(i).wait_send()
        return carry

    lax.fori_loop(0, 8, forward_done, 0)
    for n, h in pieces:
        ghost_copy_of(n, h).wait_recv()
        share_copy_of(n, h, s).start()
    for n, h in pieces:
        share_copy_of(n, h, 1 - s).wait_recv()
        unpack(n, h)

    def pull(n, idx_s):
        i0 = n * UNROLL
        b = i0 // LANE
        t0 = lax.rem(i0, LANE)
        q0 = (t0 // 32) * LANE + b * 32 + lax.rem(t0, 32)
        taken = [
            jnp.concatenate([table[idx_s[u, j]] for j in range(NBR)], axis=0)
            for u in range(UNROLL)
        ]
        sums = [
            jnp.dot(weights[i0 + u], taken[u], preferred_element_type=F32) for u in range(UNROLL)
        ]
        for u in range(UNROLL):
            for g in range(5):
                total = sums[u][g * 8 : g * 8 + 8] + sums[u][40 + g * 8 : 48 + g * 8]
                pulled[pl.ds(g * 8 * PITCH + q0 + u, 8, stride=PITCH), :] = total

    def pull_two(n, carry):
        for slot, indices in enumerate((idx_a, idx_b)):
            index_copy(2 * n + slot, slot).wait()
            pull(2 * n + slot, indices)

            @pl.when(n + 1 < HALF // UNROLL // 2)
            def _():
                index_copy(2 * n + 2 + slot, slot).start()

        return carry

    lax.fori_loop(0, HALF // UNROLL // 2, pull_two, 0)

    where = {"x": x, "y": y, "z": z}
    orders = ("xyz", "yzx", "zxy")

    def device_at(axis, j):
        if axis == "x":
            return (r, (j * 2 + zl) * 2 + s)
        if axis == "y":
            return (zh * 4 + j, c)
        return ((j // 2) * 4 + y, (x * 2 + lax.rem(j, 2)) * 2 + s)

    my_lanes = pl.ds(pl.multiple_of(s * HALF, HALF), HALF)

    lane_group = lax.broadcasted_iota(jnp.int32, (16, LANE), 1) // 32
    low = lane_group < 2
    even = lax.rem(lane_group, 2) == 0

    def velocity(a, core, keep):
        def part(zz, carry):
            rows = [
                pl.ds(pl.multiple_of(((a * 3 + comp) * 4 + 2 * core + xx) * PITCH, 8), HALF)
                for comp in range(3)
                for xx in range(2)
            ]
            rhs = jnp.concatenate(
                [
                    jnp.concatenate([pulled[rows[2 * comp], :], pulled[rows[2 * comp + 1], :]], axis=1)
                    for comp in range(3)
                ],
                axis=0,
            ).astype(BF16)
            lhs = jnp.concatenate(
                [
                    modes[comp, :, :, :, my_lanes].reshape(HALF, HALF)
                    for comp in range(3)
                ],
                axis=1,
            )
            acc = jnp.dot(lhs, rhs, preferred_element_type=F32)
            for zz, yy, xx in [(i // 8, i // 2 % 4, i % 2) for i in range(16)]:
                    at = zz * 256 + yy * 64
                    rows = [
                        acc[at + 16 * g : at + 16 * g + 16, xx * LANE : xx * LANE + LANE]
                        for g in range(4)
                    ]
                    halves = [None] * 4
                    for g in range(2):
                        halves[g] = jnp.where(low, rows[g], pltpu.roll(rows[g + 2], 64, 1))
                        halves[g + 2] = jnp.where(low, pltpu.roll(rows[g], 64, 1), rows[g + 2])
                    quarters = [None] * 4
                    for g in (0, 2):
                        quarters[g] = jnp.where(even, halves[g], pltpu.roll(halves[g + 1], 32, 1))
                        quarters[g + 1] = jnp.where(even, pltpu.roll(halves[g], 96, 1), halves[g + 1])
                    for quarter, block in enumerate(quarters):
                        xl, ll = divmod(quarter, 2)
                        pos = {"x": 2 * xx + xl, "y": yy, "z": 2 * zz + ll}
                        p, q, t = (pos[axis] for axis in orders[a])
                        place = (p * 4 + q) * 4 + t
                        if keep:
                            vkeep[a, place] = block
                        else:
                            vsend[a, place] = block.astype(BF16)
            return carry

        lax.fori_loop(0, 1, part, 0)

    def core_copy(a):
        return remote(vsend.at[a], vrecv.at[a], core_send.at[a], core_recv.at[a], sib)

    def stage_copies(a, stage, src, dst, ssem, rsem, size):
        axis = orders[a][stage]
        mine = where[axis]
        copies = []
        for d in range(1, 4):
            j = lax.rem(mine + d, 4)
            copies.append(
                remote(
                    src.at[a, pl.ds(j * size, size)], dst.at[a, mine],
                    ssem.at[a, d - 1], rsem.at[a, mine], device_at(axis, j),
                )
            )
        return copies

    def stage_wait(a, stage, dst, rsem):
        axis = orders[a][stage]
        mine = where[axis]
        total = None
        for d in range(1, 4):
            j = lax.rem(mine + d, 4)
            remote(dst.at[a, j], dst.at[a, j], rsem.at[a, j], rsem.at[a, j], sib).wait_recv()
            term = dst[a, j].astype(F32)
            total = term if total is None else total + term
        return total

    def copies1(a):
        return stage_copies(a, 0, send1, recv1, s1_send, s1_recv, 16)

    def plane_copy(a, d):
        first_axis, second_axis = orders[a][1:]
        mine = where[first_axis] * 4 + where[second_axis]
        other = lax.rem(mine + d, 16)
        at = dict(where)
        at[first_axis] = other // 4
        at[second_axis] = lax.rem(other, 4)
        dev = ((at["z"] // 2) * 4 + at["y"], (at["x"] * 2 + lax.rem(at["z"], 2)) * 2 + s)
        out_copy = remote(
            part2.at[a, other], recv2.at[a, mine], s2_send.at[a, d], s2_recv.at[a, mine], dev
        )
        return out_copy, other

    def plane_wait(a, other):
        piece = recv2.at[a, other]
        remote(piece, piece, s2_send.at[a, 0], s2_recv.at[a, other], sib).wait_recv()

    def add1(a):
        core_copy(a).wait_recv()

        copies = copies1(a)
        mine = where[orders[a][0]]
        for d in (1, 3, 2, 0):
            at = pl.ds(lax.rem(mine + d, 4) * 16, 16)
            both = vkeep[a, at] + vrecv[a, at].astype(F32)
            part1[a, at] = both
            if d:
                send1[a, at] = both.astype(BF16)
                copies[d - 1].start()

    def add2(a):
        mine = where[orders[a][0]]
        total = part1[a, pl.ds(mine * 16, 16)] + stage_wait(a, 0, recv1, s1_recv)
        part2[a] = total

        def send_one(d, carry):
            plane_copy(a, d)[0].start()
            return carry

        lax.fori_loop(1, 16, send_one, 0, unroll=5)

    def add3(a):
        mine = where[orders[a][1]] * 4 + where[orders[a][2]]

        def take_one(d, total):
            other = lax.rem(mine + d, 16)
            plane_wait(a, other)
            return total + recv2[a, other]

        total = lax.fori_loop(1, 16, take_one, part2[a, mine], unroll=5)
        turned = jnp.concatenate([total, jnp.zeros((LANE - 16, LANE), F32)], axis=0).T
        out[a] = jnp.concatenate([turned[g * 32 : g * 32 + 32, :16] for g in range(4)], axis=1)

    for a in range(3):
        velocity(a, 1 - s, False)
        core_copy(a).start()
        if a:
            add1(a - 1)
        velocity(a, s, True)
    add1(2)
    for a in range(3):
        add2(a)
    for n, h in pieces:
        ghost_copy_of(n, h).wait_send()
        share_copy_of(n, h, s).wait_send()
    for a in range(3):
        core_copy(a).wait_send()
        for copy in copies1(a):
            copy.wait_send()
    for a in range(3):
        add3(a)

    for a in range(3):

        def sent_one(d, carry, a=a):
            plane_copy(a, d)[0].wait_send()
            return carry

        lax.fori_loop(1, 16, sent_one, 0, unroll=5)


def body(mode_panel, domain_sizes, ghost_send, neighbours, force_blocks, bond_vectors):
    panel = mode_panel.transpose(1, 2, 0, 3).reshape(3, 32, 8192)
    any_spec = pl.BlockSpec(memory_space=pl.ANY)
    vm = pltpu.VMEM
    dma = pltpu.SemaphoreType.DMA
    turned = pl.pallas_call(
        kernel,
        out_shape=jax.ShapeDtypeStruct((3, 32, 64), F32),
        in_specs=[any_spec, pl.BlockSpec(memory_space=pltpu.SMEM)] + [any_spec] * 4,
        out_specs=pl.BlockSpec(memory_space=vm),
        scratch_shapes=[
            vm((3, 8, 2, 32, CHIP_ATOMS), BF16),
            vm((TABLE, 16, LANE), BF16),
            vm((CHIP_ATOMS, 16, LANE), F32),
            vm((2, 144, CAP), F32),
            vm((2, 48, CAP), F32),
            vm((2, NBR, CAP), jnp.int32),
            vm((2, 2, GHOST), jnp.int32),
            vm((192, CHIP_ATOMS), F32),
            vm((NBR, CHIP_ATOMS), jnp.int32),
            vm((HALF, LANE), jnp.int32),
            pltpu.SMEM((UNROLL, LANE), jnp.int32),
            pltpu.SMEM((UNROLL, LANE), jnp.int32),
            pltpu.SMEM((2, 2, GHOST), jnp.int32),
            vm((256, LANE), F32),
            vm((HALF, 2 * WROWS, 256), BF16),
            vm((40 * PITCH, LANE), F32),
            vm((16, 48, LANE), BF16),
            vm((16, 48, LANE), BF16),
            vm((2, 2, 16, 48, LANE), BF16),
            vm((3, 64, 16, LANE), F32),
            vm((3, 64, 16, LANE), BF16),
            vm((3, 64, 16, LANE), BF16),
            vm((3, 64, 16, LANE), F32),
            vm((3, 64, 16, LANE), BF16),
            vm((3, 4, 16, 16, LANE), BF16),
            vm((3, 16, 16, LANE), F32),
            vm((3, 16, 16, LANE), F32),
            dma((5,)), dma((4,)), dma((4,)), dma((CHIPS,)), dma((CHIPS,)), dma((CHIPS,)), dma((CHIPS,)),
            dma((2, 2)), dma((2, 2)), dma((2, 2)), dma((2, 2)),
            dma((3,)), dma((3,)),
            dma((3, 3)), dma((3, 4)), dma((3, 16)), dma((3, 16)),
        ],
        compiler_params=pltpu.CompilerParams(
            collective_id=1, has_side_effects=True, vmem_limit_bytes=63 * 2**20
        ),
    )(
        panel,
        domain_sizes,
        ghost_send.reshape(2, 128),
        neighbours.reshape(16, 768),
        force_blocks.reshape(144, 768),
        bond_vectors.reshape(48, 768),
    )
    return turned.transpose(0, 2, 1)


def solution(mesh):
    return jax.shard_map(
        body,
        mesh=mesh,
        in_specs=(
            P("col", None, "row", None),
            P(),
            P(("row", "col"), None, None),
            P(("row", "col"), None, None),
            P(("row", "col"), None, None, None, None),
            P(("row", "col"), None, None, None),
        ),
        out_specs=P(None, "row", "col"),
        check_vma=False,
    )
```

```python
import jax
import jax.numpy as jnp
from jax import lax
from jax.experimental import pallas as pl
from jax.experimental.pallas import tpu as pltpu
from jax.sharding import PartitionSpec as P

MESH = pl.DeviceIdType.MESH
BF16 = jnp.bfloat16
F32 = jnp.float32

CHIPS = 64
CAP = 768
CHIP_ATOMS = 1024
HALF = 512
NBR = 16
GHOST = 128
LANE = 128
WROWS = 40
PITCH = 520
WHALF = LANE * WROWS
UNROLL = 32
STEP = 5
FROM_PREV = 1024
OWN_AFTER = 1152
OWN_BEFORE = 1280
FROM_NEXT = 1408
ZERO_ROW = 1536
TABLE = 1544


def kernel(
    panel, sizes, ghosts, nbrs, force, bond, out,
    modes, table, wide, raw_f, raw_b, raw_n, raw_g, merged, merged_n,
    idx_v, idx_a, idx_b, ghost_s, u32, weights, pulled, to_next, to_prev, gin,
    vkeep, vsend, vrecv, part1, send1, recv1, part2, recv2,
    local_sem, raw_send, raw_recv, panel_send, panel_recv, fwd_send, fwd_recv,
    ghost_send_sem, ghost_recv_sem, gfwd_send, gfwd_recv,
    core_send, core_recv, s1_send, s1_recv, s2_send, s2_recv,
):
    r = lax.axis_index("row")
    c = lax.axis_index("col")
    s = lax.rem(c, 2)
    cp = c // 2
    me = r * 8 + cp
    zh, y = r // 4, lax.rem(r, 4)
    x, zl = cp // 2, lax.rem(cp, 2)
    z = zh * 2 + zl
    sib = (r, cp * 2 + 1 - s)

    def chip_device(k):
        return (k // 8, lax.rem(k, 8) * 2 + s)

    def lanes_of(k):
        return pl.ds(pl.multiple_of(k * LANE, LANE), LANE)

    def remote(src, dst, ssem, rsem, dev):
        return pltpu.make_async_remote_copy(
            src_ref=src, dst_ref=dst, send_sem=ssem, recv_sem=rsem,
            device_id=dev, device_id_type=MESH,
        )

    barrier = pltpu.get_barrier_semaphore()
    pl.semaphore_signal(barrier, inc=1, device_id=sib, device_id_type=MESH)

    def greet(i, carry):
        k = lax.rem(me + i, CHIPS)
        pl.semaphore_signal(barrier, inc=1, device_id=chip_device(k), device_id_type=MESH)
        return carry

    lax.fori_loop(1, CHIPS, greet, 0, unroll=9)

    raws = ((force, raw_f), (bond, raw_b), (nbrs, raw_n), (ghosts, raw_g))
    own = [
        pltpu.make_async_copy(src, dst.at[s], local_sem.at[n])
        for n, (src, dst) in enumerate(raws)
    ]
    own.append(
        pltpu.make_async_copy(
            panel.at[:, :, lanes_of(me)], modes.at[:, cp, s, :, lanes_of(r)], local_sem.at[4]
        )
    )
    for copy in own:
        copy.start()
    pl.semaphore_wait(barrier, CHIPS)

    raw_copies = [
        remote(src, dst.at[s], raw_send.at[n], raw_recv.at[n], sib)
        for n, (src, dst) in enumerate(raws)
    ]
    for copy in raw_copies:
        copy.start()

    def panel_copy(i):
        k = lax.rem(me + i * STEP, CHIPS)
        return remote(
            panel.at[:, :, lanes_of(k)], modes.at[:, cp, s, :, lanes_of(r)],
            panel_send.at[i], panel_recv.at[me], chip_device(k),
        )

    def panel_start(i, carry):
        panel_copy(i).start()
        return carry

    lax.fori_loop(1, CHIPS, panel_start, 0, unroll=7)
    zero8 = jnp.zeros((8, LANE), F32)

    def clear_w(i, carry):
        pulled[pl.ds(i * 8, 8), :] = zero8
        return carry

    lax.fori_loop(0, 2 * WHALF // 8, clear_w, 0)

    for i in range(32):
        u32[pl.ds(i * 8, 8), :] = zero8
    table[pl.ds(ZERO_ROW, TABLE - ZERO_ROW)] = jnp.zeros((TABLE - ZERO_ROW, 16, LANE), BF16)
    for copy in own:
        copy.wait()
    for copy in raw_copies:
        copy.wait()
    ghost_copy = pltpu.make_async_copy(raw_g, ghost_s, local_sem.at[0])
    ghost_copy.start()

    n0 = sizes[2 * me]
    lane = lax.broadcasted_iota(jnp.int32, (8, CHIP_ATOMS), 1)
    first = lane < n0

    def merge(x0, x1):
        pad = jnp.zeros((8, CHIP_ATOMS - CAP), x0.dtype)
        a = jnp.concatenate([x0, pad], axis=1)
        b = pltpu.roll(jnp.concatenate([x1, pad], axis=1), n0, 1)
        return jnp.where(first, a, b)

    def merge_force(g, carry):
        rows = pl.ds(pl.multiple_of(g * 8, 8), 8)
        merged[rows, :] = merge(raw_f[0, rows, :], raw_f[1, rows, :])
        return carry

    def merge_bond(g, carry):
        rows = pl.ds(pl.multiple_of(g * 8, 8), 8)
        merged[pl.ds(pl.multiple_of(144 + g * 8, 8), 8), :] = merge(
            raw_b[0, rows, :], raw_b[1, rows, :]
        )
        return carry

    lax.fori_loop(0, 18, merge_force, 0)
    lax.fori_loop(0, 6, merge_bond, 0)
    for g in range(2):
        rows = pl.ds(g * 8, 8)
        merged_n[rows, :] = merge(raw_n[0, rows, :], raw_n[1, rows, :])
    for b in range(4):
        v = merged_n[:, lanes_of(2 * b + s)]
        pos = (2 * b + s) * LANE + lax.broadcasted_iota(jnp.int32, (NBR, LANE), 1)
        late = pos >= n0
        inner = v + jnp.where(late, n0, 0)
        outer = v + jnp.where(late, 512, 256)
        row = jnp.where(v < CAP, inner, jnp.where(v >= CHIP_ATOMS, ZERO_ROW, outer))
        square = jnp.concatenate([row, jnp.zeros((LANE - NBR, LANE), jnp.int32)], axis=0)
        idx_v[pl.ds(b * LANE, LANE), :] = square.T

    block_lane = lax.rem(lax.broadcasted_iota(jnp.int32, (LANE, LANE), 1), 4)

    def weights_block(b, carry):
        tile = lanes_of(2 * b + s)

        def one(ac, carry):
            a = ac // 3
            comp = lax.rem(ac, 3)
            bv = merged[pl.ds(pl.multiple_of(144 + a * 16, 16), 16), tile]
            for e in range(3):
                w = bv * merged[pl.ds(pl.multiple_of((comp * 3 + e) * 16, 16), 16), tile]
                for m in range(4):
                    for half in range(2):
                        u32[pl.ds(half * 128 + e * 4 + m, 8, stride=16), :] = w[half * 8 : half * 8 + 8]
            for half in range(2):
                t = u32[pl.ds(half * 128, 128), :].T
                for m in range(4):
                    tm = jnp.where(block_lane == m, t, 0.0)
                    for g in range(16):
                        pulled[pl.ds(half * WHALF + g * 8 * WROWS + ac * 4 + m, 8, stride=WROWS), :] = tm[g * 8 : g * 8 + 8]
            return carry

        lax.fori_loop(0, 9, one, 0)

        def pack(t, carry):
            for half in range(2):
                w = pulled[pl.ds(pl.multiple_of(half * WHALF + t * WROWS, 8), WROWS), :]
                high = w.astype(BF16).astype(F32)
                both = jnp.concatenate([high, w - high], axis=0).astype(BF16)
                weights[b * LANE + t, :, half * LANE : half * LANE + LANE] = both
            return carry

        lax.fori_loop(0, LANE, pack, 0, unroll=4)
        return carry

    lax.fori_loop(0, 4, weights_block, 0)
    ghost_copy.wait()

    def index_copy(n, slot):
        return pltpu.make_async_copy(
            idx_v.at[pl.ds(pl.multiple_of(n * UNROLL, UNROLL), UNROLL)],
            (idx_a, idx_b)[slot], local_sem.at[slot],
        )

    def clear_rows(i, carry):
        wide[i, pl.ds(12, 4), :] = jnp.zeros((4, LANE), F32)
        return carry

    lax.fori_loop(0, CHIP_ATOMS, clear_rows, 0, unroll=8)

    def half_group(rr, core):
        return modes.at[:, :, core, :, lanes_of(rr)]

    def forward_copy(rr):
        return remote(half_group(rr, s), half_group(rr, s), fwd_send.at[rr], fwd_recv.at[rr], sib)

    def build(rr, core):
        for e in range(3):
            for xh in range(2):
                v = modes[e, 4 * xh : 4 * xh + 4, core, :, lanes_of(rr)]
                vt = v.reshape(LANE, LANE).astype(F32).T
                for g in range(16):
                    at = rr * 32 + (g // 4) * 256 + (g % 4) * 8
                    wide[pl.ds(at, 8), e * 4 + xh + 2 * core, :] = vt[g * 8 : g * 8 + 8]

    def arrive(i, carry):
        rr = lax.rem(r + 7 - i, 8)

        def wait_one(cc, carry):
            ks = rr * 8 + cc

            @pl.when(ks != me)
            def _():
                chunk = modes.at[:, cc, s, :, lanes_of(rr)]
                remote(chunk, chunk, panel_send.at[0], panel_recv.at[ks], sib).wait_recv()

            return carry

        lax.fori_loop(0, 8, wait_one, 0)
        build(rr, s)
        return carry

    lax.fori_loop(0, 8, arrive, 0)

    index_copy(0, 0).start()
    index_copy(1, 1).start()

    down = lax.broadcasted_iota(jnp.int32, (48, LANE), 0)
    across = lax.broadcasted_iota(jnp.int32, (48, LANE), 1)
    six = lax.rem(down, 6)
    place48 = (down // 6) * 16 + (six // 2) * 4 + lax.rem(six, 2) + 2 * s
    shut = jnp.where(place48 == across, 1.0, 0.0).astype(BF16)
    down = lax.broadcasted_iota(jnp.int32, (LANE, 96), 0)
    across = lax.broadcasted_iota(jnp.int32, (LANE, 96), 1)
    six = lax.rem(across, 6)
    core_at = jnp.where(across < 48, s, 1 - s)
    place96 = (lax.rem(across, 48) // 6) * 16 + (six // 2) * 4 + lax.rem(six, 2) + 2 * core_at
    open_up = jnp.where(place96 == down, 1.0, 0.0).astype(BF16)

    def pack_rows(atoms):
        rows = [wide[at] for at in atoms]
        stacked = jnp.concatenate(rows, axis=0).astype(BF16)
        return jnp.dot(shut, stacked, preferred_element_type=F32).astype(BF16)

    nxt = chip_device(lax.rem(me + 1, CHIPS))
    prv = chip_device(lax.rem(me + CHIPS - 1, CHIPS))

    def ghost_copy_of(n, h):
        piece = pl.ds(h * 4, 4)
        return remote(
            (to_next, to_prev)[n].at[piece], gin.at[n, s, piece],
            ghost_send_sem.at[n, h], ghost_recv_sem.at[n, h], (nxt, prv)[n],
        )

    def share_copy_of(n, h, half):
        piece = gin.at[n, half, pl.ds(h * 4, 4)]
        return remote(piece, piece, gfwd_send.at[n, h], gfwd_recv.at[n, h], sib)

    pieces = [(n, h) for h in range(4) for n in range(2)]

    def pick(g, carry):
        to_next[g] = pack_rows([n0 + ghost_s[1, 0, g * 8 + u] for u in range(8)])
        to_prev[g] = pack_rows([ghost_s[0, 1, g * 8 + u] for u in range(8)])
        return carry

    def forward(rr, carry):
        forward_copy(rr).start()
        return carry

    for h in range(4):
        lax.fori_loop(h * 4, h * 4 + 4, pick, 0, unroll=4)
        for n in range(2):
            ghost_copy_of(n, h).start()
        lax.fori_loop(h * 2, h * 2 + 2, forward, 0)

    def finish(rr, carry):
        other = half_group(rr, 1 - s)
        remote(other, other, fwd_send.at[rr], fwd_recv.at[rr], sib).wait_recv()
        build(rr, 1 - s)
        for b in range(4):
            first_atom = pl.multiple_of(b * 256 + rr * 32, 32)
            table[pl.ds(first_atom, 32)] = wide[pl.ds(first_atom, 32)].astype(BF16)
        return carry

    lax.fori_loop(0, 8, finish, 0)

    def pick_own(g, carry):
        table[OWN_AFTER + g] = table[n0 + ghost_s[1, 1, g]]
        table[OWN_BEFORE + g] = table[ghost_s[0, 0, g]]
        return carry

    lax.fori_loop(0, GHOST, pick_own, 0, unroll=8)

    def unpack(n, h):
        base = (FROM_PREV, FROM_NEXT)[n] + h * 32

        def step(g, carry):
            both = jnp.concatenate([gin[n, s, h * 4 + g], gin[n, 1 - s, h * 4 + g]], axis=0)
            rows = jnp.dot(open_up, both, preferred_element_type=F32)
            table[pl.ds(base + g * 8, 8)] = rows.astype(BF16).reshape(8, 16, LANE)
            return carry

        lax.fori_loop(0, 4, step, 0, unroll=4)

    def panel_done(i, carry):
        panel_copy(i).wait_send()
        return carry

    lax.fori_loop(1, CHIPS, panel_done, 0, unroll=7)

    def forward_done(i, carry):
        forward_copy(i).wait_send()
        return carry

    lax.fori_loop(0, 8, forward_done, 0)
    for n, h in pieces:
        ghost_copy_of(n, h).wait_recv()
        share_copy_of(n, h, s).start()
    for n, h in pieces:
        share_copy_of(n, h, 1 - s).wait_recv()
        unpack(n, h)

    def pull(n, idx_s):
        i0 = n * UNROLL
        b = i0 // LANE
        t0 = lax.rem(i0, LANE)
        q0 = (t0 // 32) * LANE + b * 32 + lax.rem(t0, 32)
        taken = [
            jnp.concatenate([table[idx_s[u, j]] for j in range(NBR)], axis=0)
            for u in range(UNROLL)
        ]
        sums = [
            jnp.dot(weights[i0 + u], taken[u], preferred_element_type=F32) for u in range(UNROLL)
        ]
        for u in range(UNROLL):
            for g in range(5):
                total = sums[u][g * 8 : g * 8 + 8] + sums[u][40 + g * 8 : 48 + g * 8]
                pulled[pl.ds(g * 8 * PITCH + q0 + u, 8, stride=PITCH), :] = total

    def pull_two(n, carry):
        for slot, indices in enumerate((idx_a, idx_b)):
            index_copy(2 * n + slot, slot).wait()
            pull(2 * n + slot, indices)

            @pl.when(n + 1 < HALF // UNROLL // 2)
            def _():
                index_copy(2 * n + 2 + slot, slot).start()

        return carry

    lax.fori_loop(0, HALF // UNROLL // 2, pull_two, 0)

    where = {"x": x, "y": y, "z": z}
    orders = ("xyz", "yzx", "zxy")

    def device_at(axis, j):
        if axis == "x":
            return (r, (j * 2 + zl) * 2 + s)
        if axis == "y":
            return (zh * 4 + j, c)
        return ((j // 2) * 4 + y, (x * 2 + lax.rem(j, 2)) * 2 + s)

    my_lanes = pl.ds(pl.multiple_of(s * HALF, HALF), HALF)

    lane_group = lax.broadcasted_iota(jnp.int32, (16, LANE), 1) // 32
    low = lane_group < 2
    even = lax.rem(lane_group, 2) == 0

    def velocity(a, core, keep):
        def part(zz, carry):
            rows = [
                pl.ds(pl.multiple_of(((a * 3 + comp) * 4 + 2 * core + xx) * PITCH, 8), HALF)
                for comp in range(3)
                for xx in range(2)
            ]
            rhs = jnp.concatenate(
                [
                    jnp.concatenate([pulled[rows[2 * comp], :], pulled[rows[2 * comp + 1], :]], axis=1)
                    for comp in range(3)
                ],
                axis=0,
            ).astype(BF16)
            lhs = jnp.concatenate(
                [
                    modes[comp, :, :, :, my_lanes].reshape(HALF, HALF)
                    for comp in range(3)
                ],
                axis=1,
            )
            acc = jnp.dot(lhs, rhs, preferred_element_type=F32)
            for zz, yy, xx in [(i // 8, i // 2 % 4, i % 2) for i in range(16)]:
                    at = zz * 256 + yy * 64
                    rows = [
                        acc[at + 16 * g : at + 16 * g + 16, xx * LANE : xx * LANE + LANE]
                        for g in range(4)
                    ]
                    halves = [None] * 4
                    for g in range(2):
                        halves[g] = jnp.where(low, rows[g], pltpu.roll(rows[g + 2], 64, 1))
                        halves[g + 2] = jnp.where(low, pltpu.roll(rows[g], 64, 1), rows[g + 2])
                    quarters = [None] * 4
                    for g in (0, 2):
                        quarters[g] = jnp.where(even, halves[g], pltpu.roll(halves[g + 1], 32, 1))
                        quarters[g + 1] = jnp.where(even, pltpu.roll(halves[g], 96, 1), halves[g + 1])
                    for quarter, block in enumerate(quarters):
                        xl, ll = divmod(quarter, 2)
                        pos = {"x": 2 * xx + xl, "y": yy, "z": 2 * zz + ll}
                        p, q, t = (pos[axis] for axis in orders[a])
                        place = (p * 4 + q) * 4 + t
                        if keep:
                            vkeep[a, place] = block
                        else:
                            vsend[a, place] = block.astype(BF16)
            return carry

        lax.fori_loop(0, 1, part, 0)

    def core_copy(a):
        return remote(vsend.at[a], vrecv.at[a], core_send.at[a], core_recv.at[a], sib)

    def stage_copies(a, stage, src, dst, ssem, rsem, size):
        axis = orders[a][stage]
        mine = where[axis]
        copies = []
        for d in range(1, 4):
            j = lax.rem(mine + d, 4)
            copies.append(
                remote(
                    src.at[a, pl.ds(j * size, size)], dst.at[a, mine],
                    ssem.at[a, d - 1], rsem.at[a, mine], device_at(axis, j),
                )
            )
        return copies

    def stage_wait(a, stage, dst, rsem):
        axis = orders[a][stage]
        mine = where[axis]
        total = None
        for d in range(1, 4):
            j = lax.rem(mine + d, 4)
            remote(dst.at[a, j], dst.at[a, j], rsem.at[a, j], rsem.at[a, j], sib).wait_recv()
            term = dst[a, j].astype(F32)
            total = term if total is None else total + term
        return total

    def copies1(a):
        return stage_copies(a, 0, send1, recv1, s1_send, s1_recv, 16)

    def plane_copy(a, d):
        first_axis, second_axis = orders[a][1:]
        mine = where[first_axis] * 4 + where[second_axis]
        other = lax.rem(mine + d, 16)
        at = dict(where)
        at[first_axis] = other // 4
        at[second_axis] = lax.rem(other, 4)
        dev = ((at["z"] // 2) * 4 + at["y"], (at["x"] * 2 + lax.rem(at["z"], 2)) * 2 + s)
        out_copy = remote(
            part2.at[a, other], recv2.at[a, mine], s2_send.at[a, d], s2_recv.at[a, mine], dev
        )
        return out_copy, other

    def plane_wait(a, other):
        piece = recv2.at[a, other]
        remote(piece, piece, s2_send.at[a, 0], s2_recv.at[a, other], sib).wait_recv()

    def add1(a):
        core_copy(a).wait_recv()

        copies = copies1(a)
        mine = where[orders[a][0]]
        for d in (1, 3, 2, 0):
            at = pl.ds(lax.rem(mine + d, 4) * 16, 16)
            both = vkeep[a, at] + vrecv[a, at].astype(F32)
            part1[a, at] = both
            if d:
                send1[a, at] = both.astype(BF16)
                copies[d - 1].start()

    def add2(a):
        mine = where[orders[a][0]]
        total = part1[a, pl.ds(mine * 16, 16)] + stage_wait(a, 0, recv1, s1_recv)
        part2[a] = total

        def send_one(d, carry):
            plane_copy(a, d)[0].start()
            return carry

        lax.fori_loop(1, 16, send_one, 0, unroll=5)

    def add3(a):
        mine = where[orders[a][1]] * 4 + where[orders[a][2]]

        def take_one(d, total):
            other = lax.rem(mine + d, 16)
            plane_wait(a, other)
            return total + recv2[a, other]

        total = lax.fori_loop(1, 16, take_one, part2[a, mine], unroll=5)
        turned = jnp.concatenate([total, jnp.zeros((LANE - 16, LANE), F32)], axis=0).T
        out[a] = jnp.concatenate([turned[g * 32 : g * 32 + 32, :16] for g in range(4)], axis=1)

    for a in range(3):
        velocity(a, 1 - s, False)
        core_copy(a).start()
        if a:
            add1(a - 1)
        velocity(a, s, True)
    add1(2)
    for a in range(3):
        add2(a)
    for n, h in pieces:
        ghost_copy_of(n, h).wait_send()
        share_copy_of(n, h, s).wait_send()
    for a in range(3):
        core_copy(a).wait_send()
        for copy in copies1(a):
            copy.wait_send()
    for a in range(3):
        add3(a)

    for a in range(3):

        def sent_one(d, carry, a=a):
            plane_copy(a, d)[0].wait_send()
            return carry

        lax.fori_loop(1, 16, sent_one, 0, unroll=5)


def body(mode_panel, domain_sizes, ghost_send, neighbours, force_blocks, bond_vectors):
    panel = mode_panel.transpose(1, 2, 0, 3).reshape(3, 32, 8192)
    any_spec = pl.BlockSpec(memory_space=pl.ANY)
    vm = pltpu.VMEM
    dma = pltpu.SemaphoreType.DMA
    turned = pl.pallas_call(
        kernel,
        out_shape=jax.ShapeDtypeStruct((3, 32, 64), F32),
        in_specs=[any_spec, pl.BlockSpec(memory_space=pltpu.SMEM)] + [any_spec] * 4,
        out_specs=pl.BlockSpec(memory_space=vm),
        scratch_shapes=[
            vm((3, 8, 2, 32, CHIP_ATOMS), BF16),
            vm((TABLE, 16, LANE), BF16),
            vm((CHIP_ATOMS, 16, LANE), F32),
            vm((2, 144, CAP), F32),
            vm((2, 48, CAP), F32),
            vm((2, NBR, CAP), jnp.int32),
            vm((2, 2, GHOST), jnp.int32),
            vm((192, CHIP_ATOMS), F32),
            vm((NBR, CHIP_ATOMS), jnp.int32),
            vm((HALF, LANE), jnp.int32),
            pltpu.SMEM((UNROLL, LANE), jnp.int32),
            pltpu.SMEM((UNROLL, LANE), jnp.int32),
            pltpu.SMEM((2, 2, GHOST), jnp.int32),
            vm((256, LANE), F32),
            vm((HALF, 2 * WROWS, 256), BF16),
            vm((40 * PITCH, LANE), F32),
            vm((16, 48, LANE), BF16),
            vm((16, 48, LANE), BF16),
            vm((2, 2, 16, 48, LANE), BF16),
            vm((3, 64, 16, LANE), F32),
            vm((3, 64, 16, LANE), BF16),
            vm((3, 64, 16, LANE), BF16),
            vm((3, 64, 16, LANE), F32),
            vm((3, 64, 16, LANE), BF16),
            vm((3, 4, 16, 16, LANE), BF16),
            vm((3, 16, 16, LANE), F32),
            vm((3, 16, 16, LANE), F32),
            dma((5,)), dma((4,)), dma((4,)), dma((CHIPS,)), dma((CHIPS,)), dma((CHIPS,)), dma((CHIPS,)),
            dma((2, 4)), dma((2, 4)), dma((2, 4)), dma((2, 4)),
            dma((3,)), dma((3,)),
            dma((3, 3)), dma((3, 4)), dma((3, 16)), dma((3, 16)),
        ],
        compiler_params=pltpu.CompilerParams(
            collective_id=1, has_side_effects=True, vmem_limit_bytes=63 * 2**20
        ),
    )(
        panel,
        domain_sizes,
        ghost_send.reshape(2, 128),
        neighbours.reshape(16, 768),
        force_blocks.reshape(144, 768),
        bond_vectors.reshape(48, 768),
    )
    return turned.transpose(0, 2, 1)


def solution(mesh):
    return jax.shard_map(
        body,
        mesh=mesh,
        in_specs=(
            P("col", None, "row", None),
            P(),
            P(("row", "col"), None, None),
            P(("row", "col"), None, None),
            P(("row", "col"), None, None, None, None),
            P(("row", "col"), None, None, None),
        ),
        out_specs=P(None, "row", "col"),
        check_vma=False,
    )
```
